32 devices in a mesh: dp: 8 (over y, x, core), mp: 4 (over z).
Axes of the slice: x: 2, y: 2, z: 4, core: 2. Of those that a mesh axis runs over, the one named last changes fastest.
Arguments:
- hidden: bfloat16 [256, 16, 2048], P('dp', None, 'mp'), may hold values from -6 to 6
- norm_gain: bfloat16 [2048], P('mp'), may hold values from 0.099609375 to 1.8984375
- in_x: bfloat16 [2048, 4096], P('dp', 'mp'), may hold values from -0.125 to 0.125
- in_z: bfloat16 [2048, 4096], P('dp', 'mp'), may hold values from -0.125 to 0.125
- conv_weight: float32 [4, 4096], P(None, 'mp'), may hold values from -3 to 3
- conv_bias: float32 [4096], P('mp'), may hold values from -3 to 3
- x_proj: bfloat16 [4096, 160], P(('mp', 'dp')), may hold values from -0.09375 to 0.09375
- dt_proj: bfloat16 [128, 4096], P('dp', 'mp'), may hold values from -0.5 to 0.5
- dt_bias: float32 [4096], P('mp'), may hold values from -5 to -1
- a_log: float32 [16, 4096], P(None, 'mp'), may hold values from 0 to 2.77
- skip: float32 [4096], P('mp'), may hold values from 0.5 to 1.5
- out_proj: bfloat16 [4096, 2048], P('mp', 'dp'), may hold values from -0.09375 to 0.09375
- state_pool: float32 [320, 16, 4096], P('dp', None, 'mp'), may hold values from -6 to 6
- conv_pool: float32 [320, 3, 4096], P('dp', None, 'mp'), may hold values from -6 to 6
- permutation: int32 [256], P('dp'), may hold values from 0 to 255, as said below
- page_table: int32 [256], P('dp'), may hold values from 0 to 319, as said below
- accepted: int32 [256], P('dp'), may hold values from 1 to 16
Outputs:
- verified: bfloat16 [256, 16, 2048], P('dp', None, 'mp')
- new_state_pool: float32 [320, 16, 4096], P('dp', None, 'mp')
- new_conv_pool: float32 [320, 3, 4096], P('dp', None, 'mp')
The draws below stay inside these ranges and needn't reach their ends.
Inputs may be any that keep to these rules, and one draw needn't show every extreme that they name: `permutation`: A request at position j of the block of dp index d goes to position j of the block of dp index (d + o) mod 8, where the shift o depends only on j mod 8 and takes 8 different values; so each dp index sends exactly 4 requests to each of 8 dp indices and receives 32. `page_table`: the requests of dp index d use distinct slots among the 40 slots d * 40 .. (d + 1) * 40 - 1.
All inputs are finite; a program needn't handle non-finite values.
Results may differ from the reference program's by a relative error of at most 0.0065.
Values may be sent and summed in bfloat16 or wider, within the bound.
A program may use at most 128 MiB of HBM per device.

```python
import jax
import jax.numpy as jnp
from jax import lax

D = 2048
INNER = 4096
STATE = 16
RANK = 128
CONV = 4
DRAFTS = 16
REQ_DEV = 32
POOL_DEV = 40
REQUESTS = 256
SLOTS = 320
PEERS = 8
N_DP = 8


def draw_permutation(key, part):
    values = jnp.arange(N_DP, dtype=jnp.int32)
    scores = jax.random.permutation(jax.random.fold_in(key, 3), N_DP).astype(jnp.int32)
    scores = jnp.where(values == 1, -3, jnp.where(values == N_DP - 1, -2, jnp.where(values == N_DP // 2, -1, scores))).astype(jnp.int32)
    chosen = jnp.argsort(scores, stable=True)[:PEERS].astype(jnp.int32)
    mixing = jax.random.permutation(jax.random.fold_in(key, 5), PEERS).astype(jnp.int32)
    shifts = chosen[mixing]
    order = jnp.arange(REQUESTS, dtype=jnp.int32)
    source = order // REQ_DEV
    within = order % REQ_DEV
    target = (source + shifts[within % PEERS]) % N_DP
    return (target * REQ_DEV + within).astype(jnp.int32)


def draw_page_table(key, part):
    keys = jax.random.split(jax.random.fold_in(key, 7), N_DP)
    chosen = jax.vmap(lambda one_key: jax.random.permutation(one_key, POOL_DEV)[:REQ_DEV].astype(jnp.int32))(keys)
    offsets = (jnp.arange(N_DP, dtype=jnp.int32) * POOL_DEV)[:, None]
    return (chosen + offsets).reshape(REQUESTS).astype(jnp.int32)


def place_ends(entries, key, low, largest):
    longest = entries.shape.index(max(entries.shape))
    spots = []
    for shift in (0, 1):
        where = [jax.random.randint(jax.random.fold_in(key, axis), (), 0, length) for axis, length in enumerate(entries.shape)]
        where[longest] = (where[longest] + shift) % entries.shape[longest]
        spots.append(tuple(where))
    return entries.at[spots[0]].set(low).at[spots[1]].set(largest)


def block_levels(own_key, extent, shards, low, high):
    def one(position, parts):
        draws = jax.random.uniform(jax.random.fold_in(jax.random.fold_in(own_key, 6), position), (parts,), jnp.float32, low / len(shards), high / len(shards))
        return jnp.repeat(jnp.exp(draws), extent[position] // parts).reshape((-1,) + (1,) * (len(extent) - position - 1))

    factor_of = one(*shards[0])
    for cut in shards[1:]:
        factor_of = factor_of * one(*cut)
    return factor_of


def gaussian(own_key, extent, scale, most, pieces=(), kind=jnp.bfloat16):
    gain = block_levels(own_key, extent, pieces, -0.22, 0.18) if pieces else 1.0
    drawn = jax.random.normal(own_key, extent, jnp.float32) * scale * gain
    return jnp.minimum(jnp.maximum(drawn, -most), most).astype(kind)


def setup_inputs(seed: int = 0) -> dict:
    streams_of = jax.random.split(jax.random.key(seed), 18)
    return {
        "hidden": gaussian(streams_of[0], (REQUESTS, DRAFTS, D), 1.0, 6.0, ((0, 8), (2, 4))),
        "norm_gain": jnp.clip(1.0 + 0.18 * jax.random.normal(streams_of[1], (D,), jnp.float32), 0.099609375, 1.8984375).astype(jnp.bfloat16),
        "in_x": gaussian(streams_of[2], (D, INNER), D ** -0.5, 0.125, ((0, 8), (1, 4))),
        "in_z": gaussian(streams_of[3], (D, INNER), D ** -0.5, 0.125, ((0, 8), (1, 4))),
        "conv_weight": gaussian(streams_of[4], (CONV, INNER), CONV ** -0.5, 3.0, ((1, 4),), jnp.float32),
        "conv_bias": gaussian(streams_of[5], (INNER,), 0.5, 3.0, ((0, 4),), jnp.float32),
        "x_proj": gaussian(streams_of[6], (INNER, RANK + 2 * STATE), INNER ** -0.5, 0.09375, ((0, 32),)),
        "dt_proj": gaussian(streams_of[7], (RANK, INNER), RANK ** -0.5, 0.5, ((0, 8), (1, 4))),
        "dt_bias": jnp.clip(-5.0 + 4.0 * jax.random.uniform(streams_of[8], (INNER,), jnp.float32) ** block_levels(streams_of[8], (INNER,), ((0, 4),), -0.2, 0.2), -5.0, -1.0),
        "a_log": jnp.clip(2.77 * jax.random.uniform(streams_of[9], (STATE, INNER), jnp.float32) ** block_levels(streams_of[9], (STATE, INNER), ((1, 4),), -0.2, 0.2), 0.0, 2.77),
        "skip": jnp.clip(0.5 + 1.0 * jax.random.uniform(streams_of[10], (INNER,), jnp.float32) ** block_levels(streams_of[10], (INNER,), ((0, 4),), -0.2, 0.2), 0.5, 1.5),
        "out_proj": gaussian(streams_of[11], (INNER, D), INNER ** -0.5, 0.09375, ((0, 4), (1, 8))),
        "state_pool": gaussian(streams_of[12], (SLOTS, STATE, INNER), 1.0, 6.0, ((0, 8), (2, 4)), jnp.float32),
        "conv_pool": gaussian(streams_of[13], (SLOTS, CONV - 1, INNER), 1.0, 6.0, ((0, 8), (2, 4)), jnp.float32),
        "permutation": draw_permutation(jax.random.fold_in(streams_of[17], 71), 0),
        "page_table": draw_page_table(jax.random.fold_in(streams_of[17], 71), 0),
        "accepted": place_ends(jax.random.randint(streams_of[16], (REQUESTS,), 1, DRAFTS + 1), jax.random.fold_in(streams_of[16], 1), 1, DRAFTS).astype(jnp.int32),
    }


EPS = 1e-05

def layer_block(hidden, caches, accepted, norm_gain, in_x, in_z, conv_weight, conv_bias, x_proj, dt_proj, dt_bias, a_log, skip, out_proj):
    count = hidden.shape[0]
    tokens = count * DRAFTS
    rows = hidden.reshape(tokens, D).astype(jnp.float32)
    scale = lax.rsqrt(lax.optimization_barrier(jnp.mean(rows * rows, axis=1, keepdims=True)) + EPS)
    normed = (rows * scale * norm_gain.astype(jnp.float32)).astype(jnp.bfloat16)
    x_part = jnp.dot(normed, in_x, preferred_element_type=jnp.float32).astype(jnp.bfloat16)
    z_part = jnp.dot(normed, in_z, preferred_element_type=jnp.float32).astype(jnp.bfloat16)
    states = caches[:, :STATE, :]
    edges = caches[:, STATE:, :]
    padded = jnp.concatenate([edges, x_part.astype(jnp.float32).reshape(count, DRAFTS, INNER)], axis=1)
    mixed = conv_bias + jnp.zeros((count, DRAFTS, INNER), jnp.float32)
    for offset in range(CONV):
        mixed = mixed + conv_weight[offset] * padded[:, offset:offset + DRAFTS, :]
    inputs = jax.nn.silu(mixed).astype(jnp.bfloat16)
    flat_inputs = inputs.reshape(tokens, INNER)
    low = jnp.dot(flat_inputs, x_proj[:, :RANK], preferred_element_type=jnp.float32).astype(jnp.bfloat16)
    both = jnp.einsum('ks,tk->st', x_proj[:, RANK:].astype(jnp.float32), flat_inputs.astype(jnp.float32))
    delta = jax.nn.softplus(jnp.dot(low, dt_proj, preferred_element_type=jnp.float32) + dt_bias)
    delta = delta.reshape(count, DRAFTS, INNER)
    decay_rate = -jnp.exp(a_log)
    inputs_wide = inputs.astype(jnp.float32)
    driven = delta * inputs_wide
    b_time = both[:STATE].reshape(STATE, count, DRAFTS).transpose(2, 1, 0)
    c_time = both[STATE:].reshape(STATE, count, DRAFTS).transpose(2, 1, 0)

    def advance(carry, slices):
        state, kept = carry
        step_delta, step_drive, step_b, step_c, index = slices
        state = jnp.exp(step_delta[:, None, :] * decay_rate[None]) * state + step_drive[:, None, :] * step_b[:, :, None]
        output = lax.optimization_barrier(jnp.sum(state * step_c[:, :, None], axis=1))
        kept = jnp.where((accepted - 1 == index)[:, None, None], state, kept)
        return ((state, kept), output)
    (final_state, kept), outputs = lax.scan(advance, (states, states), (delta.transpose(1, 0, 2), driven.transpose(1, 0, 2), b_time, c_time, jnp.arange(DRAFTS, dtype=jnp.int32)))
    outputs = outputs.transpose(1, 0, 2)
    z_wide = z_part.astype(jnp.float32).reshape(count, DRAFTS, INNER)
    gated = ((outputs + skip * inputs_wide) * jax.nn.silu(z_wide)).astype(jnp.bfloat16).reshape(tokens, INNER)
    index = accepted[:, None].astype(jnp.int32) + jnp.arange(CONV - 1, dtype=jnp.int32)[None, :]
    new_edges = jnp.take_along_axis(padded, index[:, :, None], axis=1)
    new_caches = jnp.concatenate([kept, new_edges], axis=1)
    result = (jnp.dot(gated, out_proj, preferred_element_type=jnp.float32) + rows).astype(jnp.bfloat16)
    return (result.reshape(count, DRAFTS, D), new_caches)

def reference(hidden, norm_gain, in_x, in_z, conv_weight, conv_bias, x_proj, dt_proj, dt_bias, a_log, skip, out_proj, state_pool, conv_pool, permutation, page_table, accepted):
    caches = jnp.concatenate([state_pool[page_table], conv_pool[page_table]], axis=1)

    def run(block):
        block_hidden, block_caches, block_accept = block
        return layer_block(block_hidden, block_caches, block_accept, norm_gain, in_x, in_z, conv_weight, conv_bias, x_proj, dt_proj, dt_bias, a_log, skip, out_proj)
    home_rows, new_caches = lax.map(run, (hidden.reshape(N_DP, REQ_DEV, DRAFTS, D), caches.reshape(N_DP, REQ_DEV, STATE + CONV - 1, INNER), accepted.reshape(N_DP, REQ_DEV)))
    home_rows = home_rows.reshape(REQUESTS, DRAFTS, D)
    new_caches = new_caches.reshape(REQUESTS, STATE + CONV - 1, INNER)
    verified = jnp.zeros_like(hidden).at[permutation].set(home_rows)
    new_state_pool = state_pool.at[page_table].set(new_caches[:, :STATE])
    new_conv_pool = conv_pool.at[page_table].set(new_caches[:, STATE:])
    return (verified, new_state_pool, new_conv_pool)
```

```python
import functools

import jax
import jax.numpy as jnp
from jax import lax
from jax.experimental import pallas as pl
from jax.experimental.pallas import tpu as pltpu
from jax.sharding import PartitionSpec as P

EPS = 1e-05
LANES = 128
VMEM_BYTES = 48 * 1024 * 1024


def whole(count, smem=0):
    vmem = pl.BlockSpec(memory_space=pltpu.VMEM)
    return [pl.BlockSpec(memory_space=pltpu.SMEM)] * smem + [vmem] * (count - smem)


def conv_kernel(
    slot_ref, accepted_ref, x_ref, pool_ref, weight_ref, bias_ref, proj_ref,
    inputs_ref, partial_ref, new_pool_ref, padded,
):
    count, drafts, _ = x_ref.shape
    taps = weight_ref.shape[0]
    new_pool_ref[...] = pool_ref[...]

    def one(r, _):
        slot = slot_ref[r]
        padded[0 : taps - 1, :] = pool_ref[slot]
        padded[taps - 1 : taps - 1 + drafts, :] = x_ref[r].astype(jnp.float32)
        mixed = bias_ref[...] + weight_ref[0:1, :] * padded[0:drafts, :]
        for k in range(1, taps):
            mixed = mixed + weight_ref[k : k + 1, :] * padded[k : k + drafts, :]
        inputs_ref[r] = (mixed / (1.0 + jnp.exp(-mixed))).astype(jnp.bfloat16)
        for k in range(taps - 1):
            new_pool_ref[slot, k : k + 1, :] = padded[pl.ds(accepted_ref[r] + k, 1), :]
        return 0

    lax.fori_loop(0, count, one, 0)
    inputs = inputs_ref[...].reshape(count * drafts, -1)
    partial_ref[...] = jnp.dot(inputs, proj_ref[...], preferred_element_type=jnp.float32)


def conv_branch(x_part, conv_pool, conv_weight, conv_bias, x_proj, slot, accepted):
    count, drafts, inner = x_part.shape
    return pl.pallas_call(
        conv_kernel,
        out_shape=(
            jax.ShapeDtypeStruct(x_part.shape, jnp.bfloat16),
            jax.ShapeDtypeStruct((count * drafts, x_proj.shape[1]), jnp.float32),
            jax.ShapeDtypeStruct(conv_pool.shape, jnp.float32),
        ),
        in_specs=whole(7, smem=2),
        out_specs=tuple(whole(3)),
        scratch_shapes=[pltpu.VMEM((24, inner), jnp.float32)],
        compiler_params=pltpu.CompilerParams(vmem_limit_bytes=VMEM_BYTES),
        cost_estimate=pl.CostEstimate(flops=200_000_000, bytes_accessed=4_000_000, transcendentals=600_000),
    )(slot, accepted, x_part, conv_pool, conv_weight, conv_bias.reshape(1, -1), x_proj)


def scan_kernel(
    slot_ref, accepted_ref, low_ref, proj_ref, dt_bias_ref, a_log_ref, skip_ref,
    inputs_ref, z_ref, both_ref, pool_ref,
    gated_ref, new_pool_ref, decay, delta, drive, rows,
):
    count, drafts, inner = inputs_ref.shape
    states = a_log_ref.shape[0]
    blocks = inner // LANES
    new_pool_ref[...] = pool_ref[...]
    decay[...] = -jnp.exp(a_log_ref[...])

    def one(r, _):
        slot = slot_ref[r]
        last = accepted_ref[r] - 1
        raw = jnp.dot(low_ref[r], proj_ref[...], preferred_element_type=jnp.float32) + dt_bias_ref[...]
        step = jnp.maximum(raw, 0.0) + jnp.log1p(jnp.exp(-jnp.abs(raw)))
        delta[...] = step
        drive[...] = step * inputs_ref[r].astype(jnp.float32)
        both = both_ref[r]
        state = [pool_ref[slot, :, j * LANES : (j + 1) * LANES] for j in range(blocks)]
        kept = list(state)
        for t in range(drafts):
            column = jnp.broadcast_to(both[:, t : t + 1], (2 * states, LANES))
            b_wide, c_wide = column[:states], column[states:]
            chosen = last == t
            for j in range(blocks):
                lanes = slice(j * LANES, (j + 1) * LANES)
                grown = jnp.exp(delta[t : t + 1, lanes] * decay[:, lanes]) * state[j]
                state[j] = grown + drive[t : t + 1, lanes] * b_wide
                rows[t : t + 1, lanes] = jnp.sum(state[j] * c_wide, axis=0, keepdims=True)
                kept[j] = jnp.where(chosen, state[j], kept[j])
        for j in range(blocks):
            new_pool_ref[slot, :, j * LANES : (j + 1) * LANES] = kept[j]
        z = z_ref[r].astype(jnp.float32)
        mixed = rows[...] + skip_ref[...] * inputs_ref[r].astype(jnp.float32)
        gated_ref[r] = (mixed * (z / (1.0 + jnp.exp(-z)))).astype(jnp.bfloat16)
        return 0

    lax.fori_loop(0, count, one, 0)


def scan_branch(low, dt_proj, dt_bias, a_log, skip, inputs, z_part, both, state_pool, slot, accepted):
    count, drafts, inner = inputs.shape
    states = a_log.shape[0]
    return pl.pallas_call(
        scan_kernel,
        out_shape=(
            jax.ShapeDtypeStruct(inputs.shape, jnp.bfloat16),
            jax.ShapeDtypeStruct(state_pool.shape, jnp.float32),
        ),
        in_specs=whole(11, smem=2),
        out_specs=tuple(whole(2)),
        scratch_shapes=[
            pltpu.VMEM((states, inner), jnp.float32),
            pltpu.VMEM((drafts, inner), jnp.float32),
            pltpu.VMEM((drafts, inner), jnp.float32),
            pltpu.VMEM((drafts, inner), jnp.float32),
        ],
        compiler_params=pltpu.CompilerParams(vmem_limit_bytes=VMEM_BYTES),
        cost_estimate=pl.CostEstimate(flops=100_000_000, bytes_accessed=10_000_000, transcendentals=9_000_000),
    )(
        slot, accepted, low, dt_proj, dt_bias.reshape(1, -1), a_log, skip.reshape(1, -1),
        inputs, z_part, both, state_pool,
    )


def route(rows, permutation, count, peers):
    period = min(count, peers)
    capacity = count // period
    me = lax.axis_index("dp")
    shift = (permutation[:period] // count - me + peers) % peers
    chunks = jnp.arange(peers)
    hit = chunks[:, None] == (me + shift[None, :]) % peers
    klass = jnp.argmax(hit, axis=1)
    grouped = rows.reshape((capacity, period) + rows.shape[1:]).swapaxes(0, 1)
    sent = jnp.take(grouped, klass, axis=0)
    got = lax.all_to_all(sent, "dp", split_axis=0, concat_axis=0, tiled=True)
    source = (me - shift + peers) % peers
    placed = jnp.take(got, source, axis=0)
    return placed.swapaxes(0, 1).reshape(rows.shape)


def on_device(
    hidden, norm_gain, in_x, in_z, conv_weight, conv_bias, x_proj, dt_proj, dt_bias,
    a_log, skip, out_proj, state_pool, conv_pool, permutation, page_table, accepted,
):
    count, drafts, width_local = hidden.shape
    tokens = count * drafts
    inner_local = in_x.shape[1]
    states = a_log.shape[0]
    rank = x_proj.shape[1] - 2 * states
    slot = page_table % state_pool.shape[0]
    peers = lax.axis_size("dp")

    full = lax.all_gather(hidden, "mp", axis=2, tiled=True)
    gain = lax.all_gather(norm_gain, "mp", axis=0, tiled=True)
    x_weight = lax.all_gather(in_x, "dp", axis=0, tiled=True)
    z_weight = lax.all_gather(in_z, "dp", axis=0, tiled=True)
    x_proj = lax.all_gather(x_proj, "dp", axis=0, tiled=True)
    dt_proj = lax.all_gather(dt_proj, "dp", axis=0, tiled=True)
    out_proj = lax.all_gather(out_proj, "dp", axis=1, tiled=True)

    rows = full.reshape(tokens, -1).astype(jnp.float32)
    scale = lax.rsqrt(jnp.mean(rows * rows, axis=1, keepdims=True) + EPS)
    normed = (rows * scale * gain.astype(jnp.float32)).astype(jnp.bfloat16)
    x_part = jnp.dot(normed, x_weight, preferred_element_type=jnp.float32).astype(jnp.bfloat16)
    z_part = jnp.dot(normed, z_weight, preferred_element_type=jnp.float32).astype(jnp.bfloat16)
    x_part = x_part.reshape(count, drafts, inner_local)
    z_part = z_part.reshape(count, drafts, inner_local)

    inputs, partial, new_conv_pool = conv_branch(
        x_part, conv_pool, conv_weight, conv_bias, x_proj, slot, accepted
    )
    summed = lax.psum(partial, "mp")
    low = summed[:, :rank].astype(jnp.bfloat16).reshape(count, drafts, rank)
    both = summed[:, rank:].reshape(count, drafts, 2 * states).transpose(0, 2, 1)
    gated, new_state_pool = scan_branch(
        low, dt_proj, dt_bias, a_log, skip, inputs, z_part, both, state_pool, slot, accepted
    )
    terms = jnp.dot(gated.reshape(tokens, inner_local), out_proj, preferred_element_type=jnp.float32)
    layer = lax.psum_scatter(terms, "mp", scatter_dimension=1, tiled=True)
    layer = (layer + hidden.reshape(tokens, width_local).astype(jnp.float32)).astype(jnp.bfloat16)
    verified = route(layer.reshape(count, drafts, width_local), permutation, count, peers)
    return (verified, new_state_pool, new_conv_pool)


def solution(mesh):
    return jax.shard_map(
        on_device,
        mesh=mesh,
        in_specs=(
            P("dp", None, "mp"),
            P("mp"),
            P("dp", "mp"),
            P("dp", "mp"),
            P(None, "mp"),
            P("mp"),
            P(("mp", "dp"), None),
            P("dp", "mp"),
            P("mp"),
            P(None, "mp"),
            P("mp"),
            P("mp", "dp"),
            P("dp", None, "mp"),
            P("dp", None, "mp"),
            P("dp"),
            P("dp"),
            P("dp"),
        ),
        out_specs=(P("dp", None, "mp"), P("dp", None, "mp"), P("dp", None, "mp")),
        check_vma=False,
    )
```

```python
import functools

import jax
import jax.numpy as jnp
from jax import lax
from jax.experimental import pallas as pl
from jax.experimental.pallas import tpu as pltpu
from jax.sharding import PartitionSpec as P

EPS = 1e-05
LANES = 128
VMEM_BYTES = 48 * 1024 * 1024


def whole(count, smem=0):
    vmem = pl.BlockSpec(memory_space=pltpu.VMEM)
    return [pl.BlockSpec(memory_space=pltpu.SMEM)] * smem + [vmem] * (count - smem)


def conv_kernel(
    slot_ref, accepted_ref, x_ref, pool_ref, weight_ref, bias_ref, proj_ref,
    inputs_ref, partial_ref, new_pool_ref, padded,
):
    count, drafts, _ = x_ref.shape
    taps = weight_ref.shape[0]
    new_pool_ref[...] = pool_ref[...]

    def one(r, _):
        slot = slot_ref[r]
        padded[0 : taps - 1, :] = pool_ref[slot]
        padded[taps - 1 : taps - 1 + drafts, :] = x_ref[r].astype(jnp.float32)
        mixed = bias_ref[...] + weight_ref[0:1, :] * padded[0:drafts, :]
        for k in range(1, taps):
            mixed = mixed + weight_ref[k : k + 1, :] * padded[k : k + drafts, :]
        inputs_ref[r] = (mixed / (1.0 + jnp.exp(-mixed))).astype(jnp.bfloat16)
        for k in range(taps - 1):
            new_pool_ref[slot, k : k + 1, :] = padded[pl.ds(accepted_ref[r] + k, 1), :]
        return 0

    lax.fori_loop(0, count, one, 0)
    inputs = inputs_ref[...].reshape(count * drafts, -1)
    partial_ref[...] = jnp.dot(inputs, proj_ref[...], preferred_element_type=jnp.float32)


def conv_branch(x_part, conv_pool, conv_weight, conv_bias, x_proj, slot, accepted):
    count, drafts, inner = x_part.shape
    return pl.pallas_call(
        conv_kernel,
        out_shape=(
            jax.ShapeDtypeStruct(x_part.shape, jnp.bfloat16),
            jax.ShapeDtypeStruct((count * drafts, x_proj.shape[1]), jnp.float32),
            jax.ShapeDtypeStruct(conv_pool.shape, jnp.float32),
        ),
        in_specs=whole(7, smem=2),
        out_specs=tuple(whole(3)),
        scratch_shapes=[pltpu.VMEM((24, inner), jnp.float32)],
        compiler_params=pltpu.CompilerParams(vmem_limit_bytes=VMEM_BYTES),
        cost_estimate=pl.CostEstimate(flops=200_000_000, bytes_accessed=4_000_000, transcendentals=600_000),
    )(slot, accepted, x_part, conv_pool, conv_weight, conv_bias.reshape(1, -1), x_proj)


def scan_kernel(
    slot_ref, accepted_ref, low_ref, proj_ref, dt_bias_ref, a_log_ref, skip_ref,
    inputs_ref, z_ref, both_ref, pool_ref,
    gated_ref, new_pool_ref, decay, delta, drive, rows,
):
    count, drafts, inner = inputs_ref.shape
    states = a_log_ref.shape[0]
    blocks = inner // LANES
    new_pool_ref[...] = pool_ref[...]
    decay[...] = -jnp.exp(a_log_ref[...])

    def one(r, _):
        slot = slot_ref[r]
        last = accepted_ref[r] - 1
        raw = jnp.dot(low_ref[r], proj_ref[...], preferred_element_type=jnp.float32) + dt_bias_ref[...]
        step = jnp.maximum(raw, 0.0) + jnp.log1p(jnp.exp(-jnp.abs(raw)))
        delta[...] = step
        drive[...] = step * inputs_ref[r].astype(jnp.float32)
        both = both_ref[r]
        state = [pool_ref[slot, :, j * LANES : (j + 1) * LANES] for j in range(blocks)]
        kept = list(state)
        for t in range(drafts):
            column = jnp.broadcast_to(both[:, t : t + 1], (2 * states, LANES))
            b_wide, c_wide = column[:states], column[states:]
            chosen = last == t
            for j in range(blocks):
                lanes = slice(j * LANES, (j + 1) * LANES)
                grown = jnp.exp(delta[t : t + 1, lanes] * decay[:, lanes]) * state[j]
                state[j] = grown + drive[t : t + 1, lanes] * b_wide
                rows[t : t + 1, lanes] = jnp.sum(state[j] * c_wide, axis=0, keepdims=True)
                kept[j] = jnp.where(chosen, state[j], kept[j])
        for j in range(blocks):
            new_pool_ref[slot, :, j * LANES : (j + 1) * LANES] = kept[j]
        z = z_ref[r].astype(jnp.float32)
        mixed = rows[...] + skip_ref[...] * inputs_ref[r].astype(jnp.float32)
        gated_ref[r] = (mixed * (z / (1.0 + jnp.exp(-z)))).astype(jnp.bfloat16)
        return 0

    lax.fori_loop(0, count, one, 0)


def scan_branch(low, dt_proj, dt_bias, a_log, skip, inputs, z_part, both, state_pool, slot, accepted):
    count, drafts, inner = inputs.shape
    states = a_log.shape[0]
    return pl.pallas_call(
        scan_kernel,
        out_shape=(
            jax.ShapeDtypeStruct(inputs.shape, jnp.bfloat16),
            jax.ShapeDtypeStruct(state_pool.shape, jnp.float32),
        ),
        in_specs=whole(11, smem=2),
        out_specs=tuple(whole(2)),
        scratch_shapes=[
            pltpu.VMEM((states, inner), jnp.float32),
            pltpu.VMEM((drafts, inner), jnp.float32),
            pltpu.VMEM((drafts, inner), jnp.float32),
            pltpu.VMEM((drafts, inner), jnp.float32),
        ],
        compiler_params=pltpu.CompilerParams(vmem_limit_bytes=VMEM_BYTES),
        cost_estimate=pl.CostEstimate(flops=100_000_000, bytes_accessed=10_000_000, transcendentals=9_000_000),
    )(
        slot, accepted, low, dt_proj, dt_bias.reshape(1, -1), a_log, skip.reshape(1, -1),
        inputs, z_part, both, state_pool,
    )


MESH = pl.DeviceIdType.MESH


def greet(partners):
    barrier = pltpu.get_barrier_semaphore()
    for partner in partners:
        pl.semaphore_signal(barrier, inc=1, device_id=partner, device_id_type=MESH)
    pl.semaphore_wait(barrier, len(partners))


def peers_on(axis, size):
    me = lax.axis_index(axis)
    return [{axis: lax.rem(me + k, size)} for k in range(1, size)]


def gather_kernel(n_mp, n_dp, *refs):
    weights = 4 if n_dp == 8 else 0
    hidden, gain = refs[0], refs[1]
    shards = refs[2 : 2 + weights]
    full, gains = refs[2 + weights], refs[3 + weights]
    wholes = refs[4 + weights : 4 + 2 * weights]
    send, recv, local = refs[4 + 2 * weights :]
    m = lax.axis_index("mp")
    width = hidden.shape[1]
    greet(peers_on("mp", n_mp) + (peers_on("dp", n_dp) if weights else []))
    made = []

    def remote(src, dst, target):
        index = len(made)
        copy = pltpu.make_async_remote_copy(
            src_ref=src, dst_ref=dst, send_sem=send.at[index], recv_sem=recv.at[index],
            device_id=target, device_id_type=MESH,
        )
        made.append(copy)
        return copy

    def started(src, dst, target):
        copy = remote(src, dst, target)
        copy.start()
        return copy

    def place(origin):
        start = pl.multiple_of(jnp.clip(origin, 0, n_mp - 1) * width, width)
        return full.at[:, pl.ds(start, width)]

    kept = []

    def keep(src, dst):
        copy = pltpu.make_async_copy(src, dst, local.at[len(kept)])
        copy.start()
        kept.append(copy)

    right, left = jnp.minimum(m + 1, n_mp - 1), jnp.maximum(m - 1, 0)
    steps = n_mp - 1
    relay = []
    for s in range(steps):
        src = hidden if s == 0 else place(m - s)
        ahead = remote(src, place(m - s), {"mp": right})
        src = hidden if s == 0 else place(m + s)
        back = remote(src, place(m + s), {"mp": left})
        relay.append((ahead, back))
    relayed = len(made)

    def sends(s):
        return (m - s >= 0) & (m + 1 < n_mp), (m + s < n_mp) & (m >= 1)

    def gets(s):
        return m - 1 - s >= 0, m + 1 + s < n_mp

    def relay_start(s):
        for copy, go in zip(relay[s], sends(s)):
            pl.when(go)(copy.start)

    def relay_arrive(s):
        for copy, go in zip(relay[s], gets(s)):
            pl.when(go)(copy.wait_recv)

    relay_start(0)
    keep(hidden, place(m))
    keep(gain, gains.at[m])
    if weights:
        d = lax.axis_index("dp")
        other = lambda bit: d + bit - 2 * bit * lax.rem(d // bit, 2)
        core, by_x, by_y = other(1), other(2), other(4)
        diagonal = by_x + 4 - 8 * lax.rem(d // 4, 2)
        own = []
        for w in range(2):
            shard, whole_w = shards[w], wholes[w]
            own.append([started(shard, whole_w.at[d], {"dp": t}) for t in (by_x, by_y, core)])
            keep(shard, whole_w.at[d])
    for k in range(1, n_mp):
        started(gain, gains.at[m], {"mp": lax.rem(m + k, n_mp)})
    if weights:
        for w in range(2, 4):
            keep(shards[w], wholes[w].at[d])
            for k in range(1, n_dp):
                started(shards[w], wholes[w].at[d], {"dp": lax.rem(d + k, n_dp)})
    relay_arrive(0)
    relay_start(1)
    done = {id(copy) for pair in relay for copy in pair}

    def arrive(copy):
        copy.wait_recv()
        done.add(id(copy))

    if weights:
        halves = []
        for w in range(2):
            whole_w = wholes[w]
            half = whole_w.shape[1] // 2
            low, high = pl.ds(0, half), pl.ds(half, half)
            arrive(own[w][0])
            first = started(whole_w.at[by_x, low], whole_w.at[by_x, low], {"dp": by_y})
            started(whole_w.at[by_x], whole_w.at[by_x], {"dp": core})
            arrive(own[w][1])
            second = started(whole_w.at[by_y, high], whole_w.at[by_y, high], {"dp": by_x})
            started(whole_w.at[by_y], whole_w.at[by_y], {"dp": core})
            halves.append((first, second))
            if w == 0:
                relay_arrive(1)
                relay_start(2)
        for w in range(2):
            whole_w = wholes[w]
            half = whole_w.shape[1] // 2
            for copy, part in zip(halves[w], (pl.ds(0, half), pl.ds(half, half))):
                arrive(copy)
                started(whole_w.at[diagonal, part], whole_w.at[diagonal, part], {"dp": core})
    else:
        relay_arrive(1)
        relay_start(2)
    relay_arrive(2)
    for copy in made:
        if id(copy) not in done:
            copy.wait_recv()
    for s in range(steps):
        for copy, go in zip(relay[s], sends(s)):
            pl.when(go)(copy.wait_send)
    for copy in made[relayed:]:
        copy.wait_send()
    for copy in kept:
        copy.wait()


def gather(hidden, gain, weights, n_mp, n_dp):
    tokens, width = hidden.shape
    gain = jnp.broadcast_to(gain[None, :], (16, width))
    shapes = [(tokens, n_mp * width), (n_mp, 16, width)] + [(n_dp,) + w.shape for w in weights]
    anywhere = pl.BlockSpec(memory_space=pl.ANY)
    copies = 2 * (n_mp - 1) + n_mp - 1 + (2 * (3 + 4 + 2) + 2 * (n_dp - 1) if weights else 0)
    return pl.pallas_call(
        functools.partial(gather_kernel, n_mp, n_dp),
        out_shape=tuple(jax.ShapeDtypeStruct(s, jnp.bfloat16) for s in shapes),
        in_specs=[anywhere] * (2 + len(weights)),
        out_specs=tuple([anywhere] * len(shapes)),
        scratch_shapes=[
            pltpu.SemaphoreType.DMA((copies,)),
            pltpu.SemaphoreType.DMA((copies,)),
            pltpu.SemaphoreType.DMA((2 + len(weights),)),
        ],
        compiler_params=pltpu.CompilerParams(collective_id=0, has_side_effects=True),
        cost_estimate=pl.CostEstimate(flops=0, bytes_accessed=100_000_000, transcendentals=0),
    )(hidden, gain, *weights)


def sum_kernel(n_mp, partial_ref, total_ref, sent, landed, send, recv):
    m = lax.axis_index("mp")
    rows = partial_ref.shape[0] // n_mp
    greet(peers_on("mp", n_mp))
    copies = []
    for k in range(1, n_mp):
        target = lax.rem(m + k, n_mp)
        piece = partial_ref[pl.ds(pl.multiple_of(target * rows, rows), rows), :]
        sent[k - 1] = piece.astype(jnp.bfloat16)
        copy = pltpu.make_async_remote_copy(
            src_ref=sent.at[k - 1], dst_ref=landed.at[k - 1], send_sem=send.at[k - 1],
            recv_sem=recv.at[k - 1], device_id={"mp": target}, device_id_type=MESH,
        )
        copy.start()
        copies.append(copy)
    mine = pl.ds(pl.multiple_of(m * rows, rows), rows)
    total = partial_ref[mine, :]
    for k in range(1, n_mp):
        copies[k - 1].wait_recv()
        total = total + landed[k - 1].astype(jnp.float32)
    total_ref[mine, :] = total.astype(jnp.bfloat16)
    spread = []
    for k in range(1, n_mp):
        copy = pltpu.make_async_remote_copy(
            src_ref=total_ref.at[mine], dst_ref=total_ref.at[mine],
            send_sem=send.at[n_mp - 2 + k], recv_sem=recv.at[n_mp - 2 + k],
            device_id={"mp": lax.rem(m + k, n_mp)}, device_id_type=MESH,
        )
        copy.start()
        spread.append(copy)
    for copy in spread:
        copy.wait_recv()
    for copy in copies + spread:
        copy.wait_send()


def sum_over_mp(partial, n_mp):
    rows, columns = partial.shape
    return pl.pallas_call(
        functools.partial(sum_kernel, n_mp),
        out_shape=jax.ShapeDtypeStruct(partial.shape, jnp.bfloat16),
        in_specs=whole(1),
        out_specs=whole(1)[0],
        scratch_shapes=[
            pltpu.VMEM((n_mp - 1, rows // n_mp, columns), jnp.bfloat16),
            pltpu.VMEM((n_mp - 1, rows // n_mp, columns), jnp.bfloat16),
            pltpu.SemaphoreType.DMA((2 * (n_mp - 1),)),
            pltpu.SemaphoreType.DMA((2 * (n_mp - 1),)),
        ],
        compiler_params=pltpu.CompilerParams(collective_id=1, has_side_effects=True),
        cost_estimate=pl.CostEstimate(flops=0, bytes_accessed=20_000_000, transcendentals=0),
    )(partial)


def output_kernel(
    n_mp, n_dp, shift_ref, class_ref, gated_ref, proj_ref, hidden_ref, out_ref,
    sent, landed, total, rows, outgoing, incoming, send, recv,
):
    m, d = lax.axis_index("mp"), lax.axis_index("dp")
    width = hidden_ref.shape[1]
    capacity, period, drafts, _ = rows.shape
    greet(peers_on("mp", n_mp) + peers_on("dp", n_dp))

    def share(target):
        columns = pl.ds(pl.multiple_of(target * width, width), width)
        return jnp.dot(gated_ref[...], proj_ref[:, columns], preferred_element_type=jnp.float32)

    copies = []
    for k in range(1, n_mp):
        target = lax.rem(m + k, n_mp)
        sent[k - 1] = share(target).astype(jnp.bfloat16)
        copy = pltpu.make_async_remote_copy(
            src_ref=sent.at[k - 1], dst_ref=landed.at[k - 1], send_sem=send.at[k - 1],
            recv_sem=recv.at[k - 1], device_id={"mp": target}, device_id_type=MESH,
        )
        copy.start()
        copies.append(copy)
    total[...] = share(m) + hidden_ref[...].astype(jnp.float32)
    for copy in copies:
        copy.wait_recv()
    layer = total[...]
    for k in range(1, n_mp):
        layer = layer + landed[k - 1].astype(jnp.float32)
    rows[...] = layer.astype(jnp.bfloat16).reshape(rows.shape)
    for o in range(n_dp):
        for c in range(capacity):
            outgoing[o, c] = rows[c, class_ref[o]]
        if o == 0:
            incoming[0] = outgoing[0]
            continue
        index = n_mp - 2 + o
        copy = pltpu.make_async_remote_copy(
            src_ref=outgoing.at[o], dst_ref=incoming.at[o], send_sem=send.at[index],
            recv_sem=recv.at[index], device_id={"dp": lax.rem(d + o, n_dp)}, device_id_type=MESH,
        )
        copy.start()
        copies.append(copy)
    for copy in copies[n_mp - 1 :]:
        copy.wait_recv()
    for k in range(period):
        for c in range(capacity):
            out_ref[c * period + k] = incoming[shift_ref[k], c]
    for copy in copies:
        copy.wait_send()


def output_branch(gated, out_proj, hidden, permutation, count, n_mp, n_dp):
    tokens, width = hidden.shape
    drafts = tokens // count
    period = min(count, n_dp)
    capacity = count // period
    shift = (permutation[:period] // count - lax.axis_index("dp") + n_dp) % n_dp
    klass = jnp.argmax(jnp.arange(n_dp)[:, None] == shift[None, :], axis=1).astype(jnp.int32)
    box = (n_dp, capacity, drafts, width)
    copies = n_mp - 1 + n_dp - 1
    return pl.pallas_call(
        functools.partial(output_kernel, n_mp, n_dp),
        out_shape=jax.ShapeDtypeStruct((count, drafts, width), jnp.bfloat16),
        in_specs=whole(5, smem=2),
        out_specs=whole(1)[0],
        scratch_shapes=[
            pltpu.VMEM((n_mp - 1, tokens, width), jnp.bfloat16),
            pltpu.VMEM((n_mp - 1, tokens, width), jnp.bfloat16),
            pltpu.VMEM((tokens, width), jnp.float32),
            pltpu.VMEM((capacity, period, drafts, width), jnp.bfloat16),
            pltpu.VMEM(box, jnp.bfloat16),
            pltpu.VMEM(box, jnp.bfloat16),
            pltpu.SemaphoreType.DMA((copies,)),
            pltpu.SemaphoreType.DMA((copies,)),
        ],
        compiler_params=pltpu.CompilerParams(
            collective_id=2, has_side_effects=True, vmem_limit_bytes=VMEM_BYTES
        ),
        cost_estimate=pl.CostEstimate(flops=2_000_000_000, bytes_accessed=100_000_000, transcendentals=0),
    )(shift.astype(jnp.int32), klass, gated, out_proj, hidden)


def on_device(
    hidden, norm_gain, in_x, in_z, conv_weight, conv_bias, x_proj, dt_proj, dt_bias,
    a_log, skip, out_proj, state_pool, conv_pool, permutation, page_table, accepted,
):
    count, drafts, width_local = hidden.shape
    tokens = count * drafts
    inner_local = in_x.shape[1]
    states = a_log.shape[0]
    rank = x_proj.shape[1] - 2 * states
    slot = page_table % state_pool.shape[0]
    n_dp, n_mp = lax.axis_size("dp"), lax.axis_size("mp")
    flat_hidden = hidden.reshape(tokens, width_local)

    out_proj = lax.all_gather(out_proj, "dp", axis=1, tiled=True)
    if n_dp == 8:
        weights = (in_x, in_z, x_proj, dt_proj)
        full, gain, *weights = gather(flat_hidden, norm_gain, weights, n_mp, n_dp)
        x_weight, z_weight, x_proj, dt_proj = [w.reshape(-1, w.shape[2]) for w in weights]
    else:
        full, gain = gather(flat_hidden, norm_gain, (), n_mp, n_dp)
        x_weight, z_weight, x_proj, dt_proj = [
            lax.all_gather(w, "dp", axis=0, tiled=True) for w in (in_x, in_z, x_proj, dt_proj)
        ]
    gain = gain[:, 0, :].reshape(-1)

    rows = full.astype(jnp.float32)
    scale = lax.rsqrt(jnp.mean(rows * rows, axis=1, keepdims=True) + EPS)
    normed = (rows * scale * gain.astype(jnp.float32)).astype(jnp.bfloat16)
    x_part = jnp.dot(normed, x_weight, preferred_element_type=jnp.float32).astype(jnp.bfloat16)
    z_part = jnp.dot(normed, z_weight, preferred_element_type=jnp.float32).astype(jnp.bfloat16)
    x_part = x_part.reshape(count, drafts, inner_local)
    z_part = z_part.reshape(count, drafts, inner_local)

    inputs, partial, new_conv_pool = conv_branch(
        x_part, conv_pool, conv_weight, conv_bias, x_proj, slot, accepted
    )
    summed = sum_over_mp(partial, n_mp)
    low = summed[:, :rank].reshape(count, drafts, rank)
    both = summed[:, rank:].astype(jnp.float32).reshape(count, drafts, 2 * states).transpose(0, 2, 1)
    gated, new_state_pool = scan_branch(
        low, dt_proj, dt_bias, a_log, skip, inputs, z_part, both, state_pool, slot, accepted
    )
    verified = output_branch(
        gated.reshape(tokens, inner_local), out_proj, flat_hidden, permutation, count, n_mp, n_dp
    )
    return (verified, new_state_pool, new_conv_pool)


def solution(mesh):
    return jax.shard_map(
        on_device,
        mesh=mesh,
        in_specs=(
            P("dp", None, "mp"),
            P("mp"),
            P("dp", "mp"),
            P("dp", "mp"),
            P(None, "mp"),
            P("mp"),
            P(("mp", "dp"), None),
            P("dp", "mp"),
            P("mp"),
            P(None, "mp"),
            P("mp"),
            P("mp", "dp"),
            P("dp", None, "mp"),
            P("dp", None, "mp"),
            P("dp"),
            P("dp"),
            P("dp"),
        ),
        out_specs=(P("dp", None, "mp"), P("dp", None, "mp"), P("dp", None, "mp")),
        check_vma=False,
    )
```

```python
import functools

import jax
import jax.numpy as jnp
from jax import lax
from jax.experimental import pallas as pl
from jax.experimental.pallas import tpu as pltpu
from jax.sharding import PartitionSpec as P

EPS = 1e-05
LANES = 128
VMEM_BYTES = 48 * 1024 * 1024


def whole(count, smem=0):
    vmem = pl.BlockSpec(memory_space=pltpu.VMEM)
    return [pl.BlockSpec(memory_space=pltpu.SMEM)] * smem + [vmem] * (count - smem)


def conv_kernel(
    slot_ref, accepted_ref, x_ref, pool_ref, weight_ref, bias_ref, proj_ref,
    inputs_ref, partial_ref, new_pool_ref, padded,
):
    count, drafts, _ = x_ref.shape
    taps = weight_ref.shape[0]
    new_pool_ref[...] = pool_ref[...]

    def one(r, _):
        slot = slot_ref[r]
        padded[0 : taps - 1, :] = pool_ref[slot]
        padded[taps - 1 : taps - 1 + drafts, :] = x_ref[r].astype(jnp.float32)
        mixed = bias_ref[...] + weight_ref[0:1, :] * padded[0:drafts, :]
        for k in range(1, taps):
            mixed = mixed + weight_ref[k : k + 1, :] * padded[k : k + drafts, :]
        inputs_ref[r] = (mixed / (1.0 + jnp.exp(-mixed))).astype(jnp.bfloat16)
        for k in range(taps - 1):
            new_pool_ref[slot, k : k + 1, :] = padded[pl.ds(accepted_ref[r] + k, 1), :]
        return 0

    lax.fori_loop(0, count, one, 0)
    inputs = inputs_ref[...].reshape(count * drafts, -1)
    partial_ref[...] = jnp.dot(inputs, proj_ref[...], preferred_element_type=jnp.float32)


def conv_branch(x_part, conv_pool, conv_weight, conv_bias, x_proj, slot, accepted):
    count, drafts, inner = x_part.shape
    return pl.pallas_call(
        conv_kernel,
        out_shape=(
            jax.ShapeDtypeStruct(x_part.shape, jnp.bfloat16),
            jax.ShapeDtypeStruct((count * drafts, x_proj.shape[1]), jnp.float32),
            jax.ShapeDtypeStruct(conv_pool.shape, jnp.float32),
        ),
        in_specs=whole(7, smem=2),
        out_specs=tuple(whole(3)),
        scratch_shapes=[pltpu.VMEM((24, inner), jnp.float32)],
        compiler_params=pltpu.CompilerParams(vmem_limit_bytes=VMEM_BYTES),
        cost_estimate=pl.CostEstimate(flops=200_000_000, bytes_accessed=4_000_000, transcendentals=600_000),
    )(slot, accepted, x_part, conv_pool, conv_weight, conv_bias.reshape(1, -1), x_proj)


MESH = pl.DeviceIdType.MESH


def greet(partners):
    barrier = pltpu.get_barrier_semaphore()
    for partner in partners:
        pl.semaphore_signal(barrier, inc=1, device_id=partner, device_id_type=MESH)
    pl.semaphore_wait(barrier, len(partners))


def peers_on(axis, size):
    me = lax.axis_index(axis)
    return [{axis: lax.rem(me + k, size)} for k in range(1, size)]


def gather_kernel(n_mp, n_dp, *refs):
    weights = 4 if n_dp == 8 else 0
    hidden, gain = refs[0], refs[1]
    shards = refs[2 : 2 + weights]
    full, gains = refs[2 + weights], refs[3 + weights]
    wholes = refs[4 + weights : 4 + 2 * weights]
    send, recv, local = refs[4 + 2 * weights :]
    m = lax.axis_index("mp")
    width = hidden.shape[1]
    greet(peers_on("mp", n_mp) + (peers_on("dp", n_dp) if weights else []))
    made = []

    def remote(src, dst, target):
        index = len(made)
        copy = pltpu.make_async_remote_copy(
            src_ref=src, dst_ref=dst, send_sem=send.at[index], recv_sem=recv.at[index],
            device_id=target, device_id_type=MESH,
        )
        made.append(copy)
        return copy

    def started(src, dst, target):
        copy = remote(src, dst, target)
        copy.start()
        return copy

    def place(origin):
        start = pl.multiple_of(jnp.clip(origin, 0, n_mp - 1) * width, width)
        return full.at[:, pl.ds(start, width)]

    kept = []

    def keep(src, dst):
        copy = pltpu.make_async_copy(src, dst, local.at[len(kept)])
        copy.start()
        kept.append(copy)

    right, left = jnp.minimum(m + 1, n_mp - 1), jnp.maximum(m - 1, 0)
    steps = n_mp - 1
    relay = []
    for s in range(steps):
        src = hidden if s == 0 else place(m - s)
        ahead = remote(src, place(m - s), {"mp": right})
        src = hidden if s == 0 else place(m + s)
        back = remote(src, place(m + s), {"mp": left})
        relay.append((ahead, back))
    relayed = len(made)

    def sends(s):
        return (m - s >= 0) & (m + 1 < n_mp), (m + s < n_mp) & (m >= 1)

    def gets(s):
        return m - 1 - s >= 0, m + 1 + s < n_mp

    def relay_start(s):
        for copy, go in zip(relay[s], sends(s)):
            pl.when(go)(copy.start)

    def relay_arrive(s):
        for copy, go in zip(relay[s], gets(s)):
            pl.when(go)(copy.wait_recv)

    relay_start(0)
    keep(hidden, place(m))
    keep(gain, gains.at[m])
    if weights:
        d = lax.axis_index("dp")
        other = lambda bit: d + bit - 2 * bit * lax.rem(d // bit, 2)
        core, by_x, by_y = other(1), other(2), other(4)
        diagonal = by_x + 4 - 8 * lax.rem(d // 4, 2)
        own = []
        for w in range(2):
            shard, whole_w = shards[w], wholes[w]
            own.append([started(shard, whole_w.at[d], {"dp": t}) for t in (by_x, by_y, core)])
            keep(shard, whole_w.at[d])
    for k in range(1, n_mp):
        started(gain, gains.at[m], {"mp": lax.rem(m + k, n_mp)})
    if weights:
        for w in range(2, 4):
            keep(shards[w], wholes[w].at[d])
            for k in range(1, n_dp):
                started(shards[w], wholes[w].at[d], {"dp": lax.rem(d + k, n_dp)})
    relay_arrive(0)
    relay_start(1)
    done = {id(copy) for pair in relay for copy in pair}

    def arrive(copy):
        copy.wait_recv()
        done.add(id(copy))

    if weights:
        halves = []
        for w in range(2):
            whole_w = wholes[w]
            half = whole_w.shape[1] // 2
            low, high = pl.ds(0, half), pl.ds(half, half)
            arrive(own[w][0])
            first = started(whole_w.at[by_x, low], whole_w.at[by_x, low], {"dp": by_y})
            started(whole_w.at[by_x], whole_w.at[by_x], {"dp": core})
            arrive(own[w][1])
            second = started(whole_w.at[by_y, high], whole_w.at[by_y, high], {"dp": by_x})
            started(whole_w.at[by_y], whole_w.at[by_y], {"dp": core})
            halves.append((first, second))
            if w == 0:
                relay_arrive(1)
                relay_start(2)
        for w in range(2):
            whole_w = wholes[w]
            half = whole_w.shape[1] // 2
            for copy, part in zip(halves[w], (pl.ds(0, half), pl.ds(half, half))):
                arrive(copy)
                started(whole_w.at[diagonal, part], whole_w.at[diagonal, part], {"dp": core})
    else:
        relay_arrive(1)
        relay_start(2)
    relay_arrive(2)
    for copy in made:
        if id(copy) not in done:
            copy.wait_recv()
    for s in range(steps):
        for copy, go in zip(relay[s], sends(s)):
            pl.when(go)(copy.wait_send)
    for copy in made[relayed:]:
        copy.wait_send()
    for copy in kept:
        copy.wait()


def gather(hidden, gain, weights, n_mp, n_dp):
    tokens, width = hidden.shape
    gain = jnp.broadcast_to(gain[None, :], (16, width))
    shapes = [(tokens, n_mp * width), (n_mp, 16, width)] + [(n_dp,) + w.shape for w in weights]
    anywhere = pl.BlockSpec(memory_space=pl.ANY)
    copies = 2 * (n_mp - 1) + n_mp - 1 + (2 * (3 + 4 + 2) + 2 * (n_dp - 1) if weights else 0)
    return pl.pallas_call(
        functools.partial(gather_kernel, n_mp, n_dp),
        out_shape=tuple(jax.ShapeDtypeStruct(s, jnp.bfloat16) for s in shapes),
        in_specs=[anywhere] * (2 + len(weights)),
        out_specs=tuple([anywhere] * len(shapes)),
        scratch_shapes=[
            pltpu.SemaphoreType.DMA((copies,)),
            pltpu.SemaphoreType.DMA((copies,)),
            pltpu.SemaphoreType.DMA((2 + len(weights),)),
        ],
        compiler_params=pltpu.CompilerParams(collective_id=0, has_side_effects=True),
        cost_estimate=pl.CostEstimate(flops=0, bytes_accessed=100_000_000, transcendentals=0),
    )(hidden, gain, *weights)


def sum_kernel(n_mp, partial_ref, normed_ref, weight_ref, total_ref, z_ref, sent, landed, send, recv):
    m = lax.axis_index("mp")
    rows = partial_ref.shape[0] // n_mp
    blocks = 4
    width = weight_ref.shape[1] // blocks

    def gate(block):
        columns = slice(block * width, (block + 1) * width)
        product = jnp.dot(normed_ref[...], weight_ref[:, columns], preferred_element_type=jnp.float32)
        z_ref[:, columns] = product.astype(jnp.bfloat16)

    greet(peers_on("mp", n_mp))
    copies = []
    for k in range(1, n_mp):
        target = lax.rem(m + k, n_mp)
        piece = partial_ref[pl.ds(pl.multiple_of(target * rows, rows), rows), :]
        sent[k - 1] = piece.astype(jnp.bfloat16)
        copy = pltpu.make_async_remote_copy(
            src_ref=sent.at[k - 1], dst_ref=landed.at[k - 1], send_sem=send.at[k - 1],
            recv_sem=recv.at[k - 1], device_id={"mp": target}, device_id_type=MESH,
        )
        copy.start()
        copies.append(copy)
    for block in range(blocks // 2):
        gate(block)
    mine = pl.ds(pl.multiple_of(m * rows, rows), rows)
    total = partial_ref[mine, :]
    for k in range(1, n_mp):
        copies[k - 1].wait_recv()
        total = total + landed[k - 1].astype(jnp.float32)
    total_ref[mine, :] = total.astype(jnp.bfloat16)
    spread = []
    for k in range(1, n_mp):
        copy = pltpu.make_async_remote_copy(
            src_ref=total_ref.at[mine], dst_ref=total_ref.at[mine],
            send_sem=send.at[n_mp - 2 + k], recv_sem=recv.at[n_mp - 2 + k],
            device_id={"mp": lax.rem(m + k, n_mp)}, device_id_type=MESH,
        )
        copy.start()
        spread.append(copy)
    for block in range(blocks // 2, blocks):
        gate(block)
    for copy in spread:
        copy.wait_recv()
    for copy in copies + spread:
        copy.wait_send()


def sum_and_gate(partial, normed, z_weight, n_mp):
    rows, columns = partial.shape
    return pl.pallas_call(
        functools.partial(sum_kernel, n_mp),
        out_shape=(
            jax.ShapeDtypeStruct(partial.shape, jnp.bfloat16),
            jax.ShapeDtypeStruct((rows, z_weight.shape[1]), jnp.bfloat16),
        ),
        in_specs=whole(3),
        out_specs=tuple(whole(2)),
        scratch_shapes=[
            pltpu.VMEM((n_mp - 1, rows // n_mp, columns), jnp.bfloat16),
            pltpu.VMEM((n_mp - 1, rows // n_mp, columns), jnp.bfloat16),
            pltpu.SemaphoreType.DMA((2 * (n_mp - 1),)),
            pltpu.SemaphoreType.DMA((2 * (n_mp - 1),)),
        ],
        compiler_params=pltpu.CompilerParams(
            collective_id=1, has_side_effects=True, vmem_limit_bytes=VMEM_BYTES
        ),
        cost_estimate=pl.CostEstimate(flops=2_000_000_000, bytes_accessed=30_000_000, transcendentals=0),
    )(partial, normed, z_weight)


def scan_kernel(
    n_mp, n_dp, shift_ref, class_ref, slot_ref, accepted_ref, holder_ref,
    low_ref, dt_proj_ref, dt_bias_ref, a_log_ref, skip_ref, inputs_ref, z_ref, pool_ref,
    proj_ref, hidden_ref,
    out_ref, new_pool_ref,
    decay, delta, drive, scanned, kept_ref, gated,
    sent, landed, total, rows, outgoing, incoming, send, recv, route_send, route_recv,
):
    m, d = lax.axis_index("mp"), lax.axis_index("dp")
    width = hidden_ref.shape[1]
    capacity, period, drafts, _ = rows.shape
    states, inner = a_log_ref.shape
    rank = dt_proj_ref.shape[0]
    part = 512
    chunk = period * drafts
    greet(peers_on("mp", n_mp) + peers_on("dp", n_dp))
    decay[...] = -jnp.exp(a_log_ref[...])

    def scan_one(r, where):
        slot = slot_ref[r]
        last = accepted_ref[r] - 1
        packed = low_ref[r]
        raw = jnp.dot(packed[:, :rank], dt_proj_ref[...], preferred_element_type=jnp.float32)
        raw = raw + dt_bias_ref[...]
        step = jnp.maximum(raw, 0.0) + jnp.log1p(jnp.exp(-jnp.abs(raw)))
        delta[...] = step
        drive[...] = step * inputs_ref[r].astype(jnp.float32)
        both = packed[:, rank:].astype(jnp.float32).T
        pieces = [slice(i, i + part) for i in range(0, inner, part)]
        state = [pool_ref[slot, :, lanes] for lanes in pieces]
        kept = list(state)
        for t in range(drafts):
            column = jnp.broadcast_to(both[:, t : t + 1], (2 * states, part))
            b_wide, c_wide = column[:states], column[states:]
            chosen = last == t
            for i, lanes in enumerate(pieces):
                grown = jnp.exp(delta[t : t + 1, lanes] * decay[:, lanes]) * state[i]
                state[i] = grown + drive[t : t + 1, lanes] * b_wide
                scanned[t : t + 1, lanes] = jnp.sum(state[i] * c_wide, axis=0, keepdims=True)
                kept[i] = jnp.where(chosen, state[i], kept[i])
        for i, lanes in enumerate(pieces):
            kept_ref[r, :, lanes] = kept[i]
        z = z_ref[r].astype(jnp.float32)
        mixed = scanned[...] + skip_ref[...] * inputs_ref[r].astype(jnp.float32)
        gated[where] = (mixed * (z / (1.0 + jnp.exp(-z)))).astype(jnp.bfloat16)

    def share(target):
        columns = pl.ds(pl.multiple_of(target * width, width), width)
        flat = gated[...].reshape(chunk, inner)
        return jnp.dot(flat, proj_ref[:, columns], preferred_element_type=jnp.float32)

    copies = []
    for c in range(capacity):

        def one(k, carry, c=c):
            scan_one(c * period + k, k)
            return carry

        lax.fori_loop(0, period, one, 0)
        for k in range(1, n_mp):
            target = lax.rem(m + k, n_mp)
            index = c * (n_mp - 1) + k - 1
            sent[index] = share(target).astype(jnp.bfloat16)
            copy = pltpu.make_async_remote_copy(
                src_ref=sent.at[index], dst_ref=landed.at[index], send_sem=send.at[index],
                recv_sem=recv.at[index], device_id={"mp": target}, device_id_type=MESH,
            )
            copy.start()
            copies.append(copy)
        own = hidden_ref[c * chunk : (c + 1) * chunk, :].astype(jnp.float32)
        total[c] = share(m) + own

    def settle(s, carry):
        holder = holder_ref[s]
        kept = kept_ref[jnp.maximum(holder, 0)]
        new_pool_ref[s] = jnp.where(holder >= 0, kept, pool_ref[s])
        return carry

    lax.fori_loop(0, new_pool_ref.shape[0], settle, 0)
    routed = []
    for c in range(capacity):
        layer = total[c]
        for k in range(n_mp - 1):
            index = c * (n_mp - 1) + k
            copies[index].wait_recv()
            layer = layer + landed[index].astype(jnp.float32)
        rows[c] = layer.astype(jnp.bfloat16).reshape(period, drafts, width)
        for o in range(n_dp):
            if o == 0:
                incoming[c, 0] = rows[c, class_ref[0]]
                continue
            outgoing[c, o] = rows[c, class_ref[o]]
            index = c * (n_dp - 1) + o - 1
            copy = pltpu.make_async_remote_copy(
                src_ref=outgoing.at[c, o], dst_ref=incoming.at[c, o], send_sem=route_send.at[index],
                recv_sem=route_recv.at[index], device_id={"dp": lax.rem(d + o, n_dp)},
                device_id_type=MESH,
            )
            copy.start()
            routed.append(copy)
    for copy in routed:
        copy.wait_recv()
    for c in range(capacity):
        for k in range(period):
            out_ref[c * period + k] = incoming[c, shift_ref[k]]
    for copy in copies + routed:
        copy.wait_send()


def scan_and_output(
    low, dt_proj, dt_bias, a_log, skip, inputs, z_part, state_pool, out_proj, hidden,
    permutation, slot, accepted, n_mp, n_dp,
):
    tokens, width = hidden.shape
    count, drafts, inner = inputs.shape
    states, slots = a_log.shape[0], state_pool.shape[0]
    period = min(count, n_dp)
    capacity = count // period
    shift = (permutation[:period] // count - lax.axis_index("dp") + n_dp) % n_dp
    klass = jnp.argmax(jnp.arange(n_dp)[:, None] == shift[None, :], axis=1).astype(jnp.int32)
    held = slot[None, :] == jnp.arange(slots)[:, None]
    holder = jnp.max(jnp.where(held, jnp.arange(count)[None, :], -1), axis=1).astype(jnp.int32)
    box = (capacity, n_dp, drafts, width)
    sums = (capacity * (n_mp - 1), period * drafts, width)
    routes = capacity * (n_dp - 1)
    return pl.pallas_call(
        functools.partial(scan_kernel, n_mp, n_dp),
        out_shape=(
            jax.ShapeDtypeStruct((count, drafts, width), jnp.bfloat16),
            jax.ShapeDtypeStruct(state_pool.shape, jnp.float32),
        ),
        in_specs=whole(15, smem=5),
        out_specs=tuple(whole(2)),
        scratch_shapes=[
            pltpu.VMEM((states, inner), jnp.float32),
            pltpu.VMEM((drafts, inner), jnp.float32),
            pltpu.VMEM((drafts, inner), jnp.float32),
            pltpu.VMEM((drafts, inner), jnp.float32),
            pltpu.VMEM((count, states, inner), jnp.float32),
            pltpu.VMEM((period, drafts, inner), jnp.bfloat16),
            pltpu.VMEM(sums, jnp.bfloat16),
            pltpu.VMEM(sums, jnp.bfloat16),
            pltpu.VMEM((capacity, period * drafts, width), jnp.float32),
            pltpu.VMEM((capacity, period, drafts, width), jnp.bfloat16),
            pltpu.VMEM(box, jnp.bfloat16),
            pltpu.VMEM(box, jnp.bfloat16),
            pltpu.SemaphoreType.DMA((sums[0],)),
            pltpu.SemaphoreType.DMA((sums[0],)),
            pltpu.SemaphoreType.DMA((routes,)),
            pltpu.SemaphoreType.DMA((routes,)),
        ],
        compiler_params=pltpu.CompilerParams(
            collective_id=2, has_side_effects=True, vmem_limit_bytes=VMEM_BYTES
        ),
        cost_estimate=pl.CostEstimate(
            flops=3_000_000_000, bytes_accessed=150_000_000, transcendentals=9_000_000
        ),
    )(
        shift.astype(jnp.int32), klass, slot, accepted, holder,
        low, dt_proj, dt_bias.reshape(1, -1), a_log, skip.reshape(1, -1),
        inputs, z_part, state_pool, out_proj, hidden,
    )


def on_device(
    hidden, norm_gain, in_x, in_z, conv_weight, conv_bias, x_proj, dt_proj, dt_bias,
    a_log, skip, out_proj, state_pool, conv_pool, permutation, page_table, accepted,
):
    count, drafts, width_local = hidden.shape
    tokens = count * drafts
    inner_local = in_x.shape[1]
    slot = page_table % state_pool.shape[0]
    n_dp, n_mp = lax.axis_size("dp"), lax.axis_size("mp")
    flat_hidden = hidden.reshape(tokens, width_local)

    if n_dp == 8:
        weights = (in_x, in_z, x_proj, dt_proj)
        full, gain, *weights = gather(flat_hidden, norm_gain, weights, n_mp, n_dp)
        x_weight, z_weight, x_proj, dt_proj = [w.reshape(-1, w.shape[2]) for w in weights]
    else:
        full, gain = gather(flat_hidden, norm_gain, (), n_mp, n_dp)
        x_weight, z_weight, x_proj, dt_proj = [
            lax.all_gather(w, "dp", axis=0, tiled=True) for w in (in_x, in_z, x_proj, dt_proj)
        ]
    gain = gain[:, 0, :].reshape(-1)
    out_proj, full = lax.optimization_barrier((out_proj, full))
    out_proj = lax.all_gather(out_proj, "dp", axis=1, tiled=True)

    rows = full.astype(jnp.float32)
    scale = lax.rsqrt(jnp.mean(rows * rows, axis=1, keepdims=True) + EPS)
    normed = (rows * scale * gain.astype(jnp.float32)).astype(jnp.bfloat16)
    x_part = jnp.dot(normed, x_weight, preferred_element_type=jnp.float32).astype(jnp.bfloat16)
    x_part = x_part.reshape(count, drafts, inner_local)

    inputs, partial, new_conv_pool = conv_branch(
        x_part, conv_pool, conv_weight, conv_bias, x_proj, slot, accepted
    )
    summed, z_part = sum_and_gate(partial, normed, z_weight, n_mp)
    verified, new_state_pool = scan_and_output(
        summed.reshape(count, drafts, -1), dt_proj, dt_bias, a_log, skip, inputs,
        z_part.reshape(count, drafts, inner_local), state_pool, out_proj, flat_hidden,
        permutation, slot, accepted, n_mp, n_dp,
    )
    return (verified, new_state_pool, new_conv_pool)


def solution(mesh):
    return jax.shard_map(
        on_device,
        mesh=mesh,
        in_specs=(
            P("dp", None, "mp"),
            P("mp"),
            P("dp", "mp"),
            P("dp", "mp"),
            P(None, "mp"),
            P("mp"),
            P(("mp", "dp"), None),
            P("dp", "mp"),
            P("mp"),
            P(None, "mp"),
            P("mp"),
            P("mp", "dp"),
            P("dp", None, "mp"),
            P("dp", None, "mp"),
            P("dp"),
            P("dp"),
            P("dp"),
        ),
        out_specs=(P("dp", None, "mp"), P("dp", None, "mp"), P("dp", None, "mp")),
        check_vma=False,
    )
```

```python
import functools

import jax
import jax.numpy as jnp
from jax import lax
from jax.experimental import pallas as pl
from jax.experimental.pallas import tpu as pltpu
from jax.sharding import PartitionSpec as P

EPS = 1e-05
LANES = 128
VMEM_BYTES = 48 * 1024 * 1024


def whole(count, smem=0):
    vmem = pl.BlockSpec(memory_space=pltpu.VMEM)
    return [pl.BlockSpec(memory_space=pltpu.SMEM)] * smem + [vmem] * (count - smem)


def conv_kernel(
    slot_ref, accepted_ref, x_ref, pool_ref, weight_ref, bias_ref, proj_ref,
    inputs_ref, partial_ref, new_pool_ref, padded,
):
    count, drafts, _ = x_ref.shape
    taps = weight_ref.shape[0]
    new_pool_ref[...] = pool_ref[...]

    def one(r, _):
        slot = slot_ref[r]
        padded[0 : taps - 1, :] = pool_ref[slot]
        padded[taps - 1 : taps - 1 + drafts, :] = x_ref[r].astype(jnp.float32)
        mixed = bias_ref[...] + weight_ref[0:1, :] * padded[0:drafts, :]
        for k in range(1, taps):
            mixed = mixed + weight_ref[k : k + 1, :] * padded[k : k + drafts, :]
        inputs_ref[r] = (mixed / (1.0 + jnp.exp(-mixed))).astype(jnp.bfloat16)
        for k in range(taps - 1):
            new_pool_ref[slot, k : k + 1, :] = padded[pl.ds(accepted_ref[r] + k, 1), :]
        return 0

    lax.fori_loop(0, count, one, 0)
    pieces, columns, depth = proj_ref.shape
    partial_ref[...] = jnp.zeros_like(partial_ref)
    total = None
    for i in range(pieces):
        part = inputs_ref[:, :, i * depth : (i + 1) * depth].reshape(count * drafts, depth)
        term = lax.dot_general(
            part, proj_ref[i], (((1,), (1,)), ((), ())), preferred_element_type=jnp.float32
        )
        total = term if total is None else total + term
    partial_ref[:, :columns] = total


def conv_branch(x_part, conv_pool, conv_weight, conv_bias, x_proj, slot, accepted):
    count, drafts, inner = x_part.shape
    return pl.pallas_call(
        conv_kernel,
        out_shape=(
            jax.ShapeDtypeStruct(x_part.shape, jnp.bfloat16),
            jax.ShapeDtypeStruct((count * drafts, 2 * LANES), jnp.float32),
            jax.ShapeDtypeStruct(conv_pool.shape, jnp.float32),
        ),
        in_specs=whole(7, smem=2),
        out_specs=tuple(whole(3)),
        scratch_shapes=[pltpu.VMEM((24, inner), jnp.float32)],
        compiler_params=pltpu.CompilerParams(vmem_limit_bytes=VMEM_BYTES),
        cost_estimate=pl.CostEstimate(flops=200_000_000, bytes_accessed=4_000_000, transcendentals=600_000),
    )(slot, accepted, x_part, conv_pool, conv_weight, conv_bias.reshape(1, -1), x_proj)


MESH = pl.DeviceIdType.MESH


def greet(partners):
    barrier = pltpu.get_barrier_semaphore()
    for partner in partners:
        pl.semaphore_signal(barrier, inc=1, device_id=partner, device_id_type=MESH)
    pl.semaphore_wait(barrier, len(partners))


def peers_on(axis, size):
    me = lax.axis_index(axis)
    return [{axis: lax.rem(me + k, size)} for k in range(1, size)]


def gather_kernel(n_mp, n_dp, *refs):
    weights = 4 if n_dp == 8 else 0
    hidden, gain = refs[0], refs[1]
    shards = refs[2 : 2 + weights]
    full, gains = refs[2 + weights], refs[3 + weights]
    wholes = refs[4 + weights : 4 + 2 * weights]
    send, recv, local = refs[4 + 2 * weights :]
    m = lax.axis_index("mp")
    width = hidden.shape[1]
    greet(peers_on("mp", n_mp) + (peers_on("dp", n_dp) if weights else []))
    made = []

    def remote(src, dst, target):
        index = len(made)
        copy = pltpu.make_async_remote_copy(
            src_ref=src, dst_ref=dst, send_sem=send.at[index], recv_sem=recv.at[index],
            device_id=target, device_id_type=MESH,
        )
        made.append(copy)
        return copy

    def started(src, dst, target):
        copy = remote(src, dst, target)
        copy.start()
        return copy

    def place(origin):
        start = pl.multiple_of(jnp.clip(origin, 0, n_mp - 1) * width, width)
        return full.at[:, pl.ds(start, width)]

    kept = []

    def keep(src, dst):
        copy = pltpu.make_async_copy(src, dst, local.at[len(kept)])
        copy.start()
        kept.append(copy)

    right, left = jnp.minimum(m + 1, n_mp - 1), jnp.maximum(m - 1, 0)
    steps = n_mp - 1
    relay = []
    for s in range(steps):
        src = hidden if s == 0 else place(m - s)
        ahead = remote(src, place(m - s), {"mp": right})
        src = hidden if s == 0 else place(m + s)
        back = remote(src, place(m + s), {"mp": left})
        relay.append((ahead, back))
    relayed = len(made)

    def sends(s):
        return (m - s >= 0) & (m + 1 < n_mp), (m + s < n_mp) & (m >= 1)

    def gets(s):
        return m - 1 - s >= 0, m + 1 + s < n_mp

    def relay_start(s):
        for copy, go in zip(relay[s], sends(s)):
            pl.when(go)(copy.start)

    def relay_arrive(s):
        for copy, go in zip(relay[s], gets(s)):
            pl.when(go)(copy.wait_recv)

    relay_start(0)
    keep(hidden, place(m))
    keep(gain, gains.at[m])
    if weights:
        d = lax.axis_index("dp")
        other = lambda bit: d + bit - 2 * bit * lax.rem(d // bit, 2)
        core, by_x, by_y = other(1), other(2), other(4)
        diagonal = by_x + 4 - 8 * lax.rem(d // 4, 2)
        own = []
        for w in range(2):
            shard, whole_w = shards[w], wholes[w]
            own.append([started(shard, whole_w.at[d], {"dp": t}) for t in (by_x, by_y, core)])
            keep(shard, whole_w.at[d])
    for k in range(1, n_mp):
        started(gain, gains.at[m], {"mp": lax.rem(m + k, n_mp)})
    if weights:
        for w in range(2, 4):
            keep(shards[w], wholes[w].at[d])
            for k in range(1, n_dp):
                started(shards[w], wholes[w].at[d], {"dp": lax.rem(d + k, n_dp)})
    relay_arrive(0)
    relay_start(1)
    done = {id(copy) for pair in relay for copy in pair}

    def arrive(copy):
        copy.wait_recv()
        done.add(id(copy))

    if weights:
        halves = []
        for w in range(2):
            whole_w = wholes[w]
            half = whole_w.shape[1] // 2
            low, high = pl.ds(0, half), pl.ds(half, half)
            arrive(own[w][0])
            first = started(whole_w.at[by_x, low], whole_w.at[by_x, low], {"dp": by_y})
            started(whole_w.at[by_x], whole_w.at[by_x], {"dp": core})
            arrive(own[w][1])
            second = started(whole_w.at[by_y, high], whole_w.at[by_y, high], {"dp": by_x})
            started(whole_w.at[by_y], whole_w.at[by_y], {"dp": core})
            halves.append((first, second))
            if w == 0:
                relay_arrive(1)
                relay_start(2)
        for w in range(2):
            whole_w = wholes[w]
            half = whole_w.shape[1] // 2
            for copy, part in zip(halves[w], (pl.ds(0, half), pl.ds(half, half))):
                arrive(copy)
                started(whole_w.at[diagonal, part], whole_w.at[diagonal, part], {"dp": core})
    else:
        relay_arrive(1)
        relay_start(2)
    relay_arrive(2)
    for copy in made:
        if id(copy) not in done:
            copy.wait_recv()
    for s in range(steps):
        for copy, go in zip(relay[s], sends(s)):
            pl.when(go)(copy.wait_send)
    for copy in made[relayed:]:
        copy.wait_send()
    for copy in kept:
        copy.wait()


def gather(hidden, gain, weights, n_mp, n_dp):
    tokens, width = hidden.shape
    gain = jnp.broadcast_to(gain[None, :], (16, width))
    shapes = [(tokens, n_mp * width), (n_mp, 16, width)] + [(n_dp,) + w.shape for w in weights]
    anywhere = pl.BlockSpec(memory_space=pl.ANY)
    copies = 2 * (n_mp - 1) + n_mp - 1 + (2 * (3 + 4 + 2) + 2 * (n_dp - 1) if weights else 0)
    return pl.pallas_call(
        functools.partial(gather_kernel, n_mp, n_dp),
        out_shape=tuple(jax.ShapeDtypeStruct(s, jnp.bfloat16) for s in shapes),
        in_specs=[anywhere] * (2 + len(weights)),
        out_specs=tuple([anywhere] * len(shapes)),
        scratch_shapes=[
            pltpu.SemaphoreType.DMA((copies,)),
            pltpu.SemaphoreType.DMA((copies,)),
            pltpu.SemaphoreType.DMA((2 + len(weights),)),
        ],
        compiler_params=pltpu.CompilerParams(collective_id=0, has_side_effects=True),
        cost_estimate=pl.CostEstimate(flops=0, bytes_accessed=100_000_000, transcendentals=0),
    )(hidden, gain, *weights)


def sum_kernel(n_mp, partial_ref, normed_ref, weight_ref, total_ref, z_ref, sent, landed, send, recv):
    m = lax.axis_index("mp")
    rows = partial_ref.shape[0] // n_mp
    blocks = 4
    width = weight_ref.shape[1] // blocks

    def gate(block):
        columns = slice(block * width, (block + 1) * width)
        product = jnp.dot(normed_ref[...], weight_ref[:, columns], preferred_element_type=jnp.float32)
        z_ref[:, columns] = product.astype(jnp.bfloat16)

    greet(peers_on("mp", n_mp))
    copies = []
    for k in range(1, n_mp):
        target = lax.rem(m + k, n_mp)
        piece = partial_ref[pl.ds(pl.multiple_of(target * rows, rows), rows), :]
        sent[k - 1] = piece.astype(jnp.bfloat16)
        copy = pltpu.make_async_remote_copy(
            src_ref=sent.at[k - 1], dst_ref=landed.at[k - 1], send_sem=send.at[k - 1],
            recv_sem=recv.at[k - 1], device_id={"mp": target}, device_id_type=MESH,
        )
        copy.start()
        copies.append(copy)
    for block in range(blocks // 2):
        gate(block)
    mine = pl.ds(pl.multiple_of(m * rows, rows), rows)
    total = partial_ref[mine, :]
    for k in range(1, n_mp):
        copies[k - 1].wait_recv()
        total = total + landed[k - 1].astype(jnp.float32)
    total_ref[mine, :] = total.astype(jnp.bfloat16)
    spread = []
    for k in range(1, n_mp):
        copy = pltpu.make_async_remote_copy(
            src_ref=total_ref.at[mine], dst_ref=total_ref.at[mine],
            send_sem=send.at[n_mp - 2 + k], recv_sem=recv.at[n_mp - 2 + k],
            device_id={"mp": lax.rem(m + k, n_mp)}, device_id_type=MESH,
        )
        copy.start()
        spread.append(copy)
    for block in range(blocks // 2, blocks):
        gate(block)
    for copy in spread:
        copy.wait_recv()
    for copy in copies + spread:
        copy.wait_send()


def sum_and_gate(partial, normed, z_weight, n_mp):
    rows, columns = partial.shape
    return pl.pallas_call(
        functools.partial(sum_kernel, n_mp),
        out_shape=(
            jax.ShapeDtypeStruct(partial.shape, jnp.bfloat16),
            jax.ShapeDtypeStruct((rows, z_weight.shape[1]), jnp.bfloat16),
        ),
        in_specs=whole(3),
        out_specs=tuple(whole(2)),
        scratch_shapes=[
            pltpu.VMEM((n_mp - 1, rows // n_mp, columns), jnp.bfloat16),
            pltpu.VMEM((n_mp - 1, rows // n_mp, columns), jnp.bfloat16),
            pltpu.SemaphoreType.DMA((2 * (n_mp - 1),)),
            pltpu.SemaphoreType.DMA((2 * (n_mp - 1),)),
        ],
        compiler_params=pltpu.CompilerParams(
            collective_id=1, has_side_effects=True, vmem_limit_bytes=VMEM_BYTES
        ),
        cost_estimate=pl.CostEstimate(flops=2_000_000_000, bytes_accessed=30_000_000, transcendentals=0),
    )(partial, normed, z_weight)


def scan_kernel(
    n_mp, n_dp, shift_ref, class_ref, slot_ref, accepted_ref, holder_ref,
    low_ref, dt_proj_ref, dt_bias_ref, a_log_ref, skip_ref, inputs_ref, z_ref, pool_ref,
    proj_ref, hidden_ref,
    out_ref, new_pool_ref,
    decay, delta, drive, scanned, kept_ref, gated,
    sent, landed, relay_out, relay_in, far_own, far_sent, far_landed, total, rows, outgoing, incoming,
    send, recv, relay_send, relay_recv, far_send, far_recv, route_send, route_recv,
):
    m, d = lax.axis_index("mp"), lax.axis_index("dp")
    width = hidden_ref.shape[1]
    capacity, period, drafts, _ = rows.shape
    states, inner = a_log_ref.shape
    rank = dt_proj_ref.shape[0]
    part = 512
    chunk = period * drafts
    greet(peers_on("mp", n_mp) + peers_on("dp", n_dp))
    decay[...] = -jnp.exp(a_log_ref[...])

    def scan_one(r, where):
        slot = slot_ref[r]
        last = accepted_ref[r] - 1
        packed = low_ref[r]
        raw = jnp.dot(packed[:, :rank], dt_proj_ref[...], preferred_element_type=jnp.float32)
        raw = raw + dt_bias_ref[...]
        step = jnp.maximum(raw, 0.0) + jnp.log1p(jnp.exp(-jnp.abs(raw)))
        delta[...] = step
        drive[...] = step * inputs_ref[r].astype(jnp.float32)
        both = packed[:, rank : rank + 2 * states].astype(jnp.float32).T
        pieces = [slice(i, i + part) for i in range(0, inner, part)]
        state = [pool_ref[slot, :, lanes] for lanes in pieces]
        kept = list(state)
        for t in range(drafts):
            column = jnp.broadcast_to(both[:, t : t + 1], (2 * states, part))
            b_wide, c_wide = column[:states], column[states:]
            chosen = last == t
            for i, lanes in enumerate(pieces):
                grown = jnp.exp(delta[t : t + 1, lanes] * decay[:, lanes]) * state[i]
                state[i] = grown + drive[t : t + 1, lanes] * b_wide
                scanned[t : t + 1, lanes] = jnp.sum(state[i] * c_wide, axis=0, keepdims=True)
                kept[i] = jnp.where(chosen, state[i], kept[i])
        for i, lanes in enumerate(pieces):
            kept_ref[r, :, lanes] = kept[i]
        z = z_ref[r].astype(jnp.float32)
        mixed = scanned[...] + skip_ref[...] * inputs_ref[r].astype(jnp.float32)
        gated[where] = (mixed * (z / (1.0 + jnp.exp(-z)))).astype(jnp.bfloat16)

    def share(target):
        columns = pl.ds(pl.multiple_of(target * width, width), width)
        flat = gated[...].reshape(chunk, inner)
        return jnp.dot(flat, proj_ref[:, columns], preferred_element_type=jnp.float32)

    partner = m + 1 - 2 * lax.rem(m, 2)
    far = 2 - 2 * (m // 2)
    is_end = (m == 0) | (m == n_mp - 1)
    is_inner = (m > 0) & (m < n_mp - 1)
    copies, relays, fars = [], [], []

    def remote(src, dst, send_sem, recv_sem, target):
        return pltpu.make_async_remote_copy(
            src_ref=src, dst_ref=dst, send_sem=send_sem, recv_sem=recv_sem,
            device_id={"mp": target}, device_id_type=MESH,
        )

    def pass_on(c):
        @pl.when(is_inner)
        def _():
            for j in range(2):
                relays[c][j].wait_recv()
                mixed = far_own[c % 2, j] + relay_in[c, j].astype(jnp.float32)
                far_sent[c, j] = mixed.astype(jnp.bfloat16)
                fars[c][j].start()

    for c in range(capacity):

        def one(k, carry, c=c):
            scan_one(c * period + k, k)
            return carry

        lax.fori_loop(0, period, one, 0)
        relays.append([
            remote(relay_out.at[c, j], relay_in.at[c, j], relay_send.at[c, j], relay_recv.at[c, j], partner)
            for j in range(2)
        ])
        fars.append([
            remote(far_sent.at[c, j], far_landed.at[c], far_send.at[c, j], far_recv.at[c], far + j)
            for j in range(2)
        ])
        for j in range(2):
            far_own[c % 2, j] = share(far + j)

            @pl.when(is_end)
            def _():
                relay_out[c, j] = far_own[c % 2, j].astype(jnp.bfloat16)
                relays[c][j].start()

        sent[c] = share(partner).astype(jnp.bfloat16)
        copies.append(remote(sent.at[c], landed.at[c], send.at[c], recv.at[c], partner))
        copies[c].start()
        own = hidden_ref[c * chunk : (c + 1) * chunk, :].astype(jnp.float32)
        total[c] = share(m) + own
        if c > 0:
            pass_on(c - 1)
    pass_on(capacity - 1)

    def settle(s, carry):
        holder = holder_ref[s]
        kept = kept_ref[jnp.maximum(holder, 0)]
        new_pool_ref[s] = jnp.where(holder >= 0, kept, pool_ref[s])
        return carry

    lax.fori_loop(0, new_pool_ref.shape[0], settle, 0)
    routed = []
    for c in range(capacity):
        copies[c].wait_recv()
        fars[c][0].wait_recv()
        layer = total[c] + landed[c].astype(jnp.float32) + far_landed[c].astype(jnp.float32)
        rows[c] = layer.astype(jnp.bfloat16).reshape(period, drafts, width)
        for o in range(n_dp):
            if o == 0:
                incoming[c, 0] = rows[c, class_ref[0]]
                continue
            outgoing[c, o] = rows[c, class_ref[o]]
            index = c * (n_dp - 1) + o - 1
            copy = pltpu.make_async_remote_copy(
                src_ref=outgoing.at[c, o], dst_ref=incoming.at[c, o], send_sem=route_send.at[index],
                recv_sem=route_recv.at[index], device_id={"dp": lax.rem(d + o, n_dp)},
                device_id_type=MESH,
            )
            copy.start()
            routed.append(copy)
    for copy in routed:
        copy.wait_recv()
    for c in range(capacity):
        for k in range(period):
            out_ref[c * period + k] = incoming[c, shift_ref[k]]
    for copy in copies + routed:
        copy.wait_send()
    for c in range(capacity):
        for j in range(2):
            pl.when(is_end)(relays[c][j].wait_send)
            pl.when(is_inner)(fars[c][j].wait_send)


def scan_and_output(
    low, dt_proj, dt_bias, a_log, skip, inputs, z_part, state_pool, out_proj, hidden,
    permutation, slot, accepted, n_mp, n_dp,
):
    tokens, width = hidden.shape
    count, drafts, inner = inputs.shape
    states, slots = a_log.shape[0], state_pool.shape[0]
    period = min(count, n_dp)
    capacity = count // period
    shift = (permutation[:period] // count - lax.axis_index("dp") + n_dp) % n_dp
    klass = jnp.argmax(jnp.arange(n_dp)[:, None] == shift[None, :], axis=1).astype(jnp.int32)
    held = slot[None, :] == jnp.arange(slots)[:, None]
    holder = jnp.max(jnp.where(held, jnp.arange(count)[None, :], -1), axis=1).astype(jnp.int32)
    box = (capacity, n_dp, drafts, width)
    piece = (period * drafts, width)
    routes = capacity * (n_dp - 1)
    return pl.pallas_call(
        functools.partial(scan_kernel, n_mp, n_dp),
        out_shape=(
            jax.ShapeDtypeStruct((count, drafts, width), jnp.bfloat16),
            jax.ShapeDtypeStruct(state_pool.shape, jnp.float32),
        ),
        in_specs=whole(15, smem=5),
        out_specs=tuple(whole(2)),
        scratch_shapes=[
            pltpu.VMEM((states, inner), jnp.float32),
            pltpu.VMEM((drafts, inner), jnp.float32),
            pltpu.VMEM((drafts, inner), jnp.float32),
            pltpu.VMEM((drafts, inner), jnp.float32),
            pltpu.VMEM((count, states, inner), jnp.float32),
            pltpu.VMEM((period, drafts, inner), jnp.bfloat16),
            pltpu.VMEM((capacity,) + piece, jnp.bfloat16),
            pltpu.VMEM((capacity,) + piece, jnp.bfloat16),
            pltpu.VMEM((capacity, 2) + piece, jnp.bfloat16),
            pltpu.VMEM((capacity, 2) + piece, jnp.bfloat16),
            pltpu.VMEM((2, 2) + piece, jnp.float32),
            pltpu.VMEM((capacity, 2) + piece, jnp.bfloat16),
            pltpu.VMEM((capacity,) + piece, jnp.bfloat16),
            pltpu.VMEM((capacity, period * drafts, width), jnp.float32),
            pltpu.VMEM((capacity, period, drafts, width), jnp.bfloat16),
            pltpu.VMEM(box, jnp.bfloat16),
            pltpu.VMEM(box, jnp.bfloat16),
            pltpu.SemaphoreType.DMA((capacity,)),
            pltpu.SemaphoreType.DMA((capacity,)),
            pltpu.SemaphoreType.DMA((capacity, 2)),
            pltpu.SemaphoreType.DMA((capacity, 2)),
            pltpu.SemaphoreType.DMA((capacity, 2)),
            pltpu.SemaphoreType.DMA((capacity,)),
            pltpu.SemaphoreType.DMA((routes,)),
            pltpu.SemaphoreType.DMA((routes,)),
        ],
        compiler_params=pltpu.CompilerParams(
            collective_id=2, has_side_effects=True, vmem_limit_bytes=VMEM_BYTES
        ),
        cost_estimate=pl.CostEstimate(
            flops=3_000_000_000, bytes_accessed=150_000_000, transcendentals=9_000_000
        ),
    )(
        shift.astype(jnp.int32), klass, slot, accepted, holder,
        low, dt_proj, dt_bias.reshape(1, -1), a_log, skip.reshape(1, -1),
        inputs, z_part, state_pool, out_proj, hidden,
    )


def on_device(
    hidden, norm_gain, in_x, in_z, conv_weight, conv_bias, x_proj, dt_proj, dt_bias,
    a_log, skip, out_proj, state_pool, conv_pool, permutation, page_table, accepted,
):
    count, drafts, width_local = hidden.shape
    tokens = count * drafts
    inner_local = in_x.shape[1]
    slot = page_table % state_pool.shape[0]
    n_dp, n_mp = lax.axis_size("dp"), lax.axis_size("mp")
    flat_hidden = hidden.reshape(tokens, width_local)

    if n_dp == 8:
        weights = (in_x, in_z, x_proj.T, dt_proj)
        full, gain, *weights = gather(flat_hidden, norm_gain, weights, n_mp, n_dp)
        x_weight, z_weight, _, dt_proj = [w.reshape(-1, w.shape[2]) for w in weights]
        x_proj = weights[2]
    else:
        full, gain = gather(flat_hidden, norm_gain, (), n_mp, n_dp)
        x_weight, z_weight, x_proj, dt_proj = [
            lax.all_gather(w, "dp", axis=0, tiled=True) for w in (in_x, in_z, x_proj, dt_proj)
        ]
        x_proj = x_proj.T[None]
    gain = gain[:, 0, :].reshape(-1)
    out_proj, full = lax.optimization_barrier((out_proj, full))
    out_proj = lax.all_gather(out_proj, "dp", axis=1, tiled=True)

    rows = full.astype(jnp.float32)
    scale = lax.rsqrt(jnp.mean(rows * rows, axis=1, keepdims=True) + EPS)
    normed = (rows * scale * gain.astype(jnp.float32)).astype(jnp.bfloat16)
    x_part = jnp.dot(normed, x_weight, preferred_element_type=jnp.float32).astype(jnp.bfloat16)
    x_part = x_part.reshape(count, drafts, inner_local)

    inputs, partial, new_conv_pool = conv_branch(
        x_part, conv_pool, conv_weight, conv_bias, x_proj, slot, accepted
    )
    summed, z_part = sum_and_gate(partial, normed, z_weight, n_mp)
    verified, new_state_pool = scan_and_output(
        summed.reshape(count, drafts, -1), dt_proj, dt_bias, a_log, skip, inputs,
        z_part.reshape(count, drafts, inner_local), state_pool, out_proj, flat_hidden,
        permutation, slot, accepted, n_mp, n_dp,
    )
    return (verified, new_state_pool, new_conv_pool)


def solution(mesh):
    return jax.shard_map(
        on_device,
        mesh=mesh,
        in_specs=(
            P("dp", None, "mp"),
            P("mp"),
            P("dp", "mp"),
            P("dp", "mp"),
            P(None, "mp"),
            P("mp"),
            P(("mp", "dp"), None),
            P("dp", "mp"),
            P("mp"),
            P(None, "mp"),
            P("mp"),
            P("mp", "dp"),
            P("dp", None, "mp"),
            P("dp", None, "mp"),
            P("dp"),
            P("dp"),
            P("dp"),
        ),
        out_specs=(P("dp", None, "mp"), P("dp", None, "mp"), P("dp", None, "mp")),
        check_vma=False,
    )
```

```python
import functools

import jax
import jax.numpy as jnp
from jax import lax
from jax.experimental import pallas as pl
from jax.experimental.pallas import tpu as pltpu
from jax.sharding import PartitionSpec as P

EPS = 1e-05
LANES = 128
VMEM_BYTES = 48 * 1024 * 1024


def whole(count, smem=0):
    vmem = pl.BlockSpec(memory_space=pltpu.VMEM)
    return [pl.BlockSpec(memory_space=pltpu.SMEM)] * smem + [vmem] * (count - smem)


def conv_kernel(
    slot_ref, accepted_ref, x_ref, pool_ref, weight_ref, bias_ref, proj_ref,
    inputs_ref, partial_ref, new_pool_ref, padded,
):
    count, drafts, _ = x_ref.shape
    taps = weight_ref.shape[0]
    new_pool_ref[...] = pool_ref[...]

    def one(r, _):
        slot = slot_ref[r]
        padded[0 : taps - 1, :] = pool_ref[slot]
        padded[taps - 1 : taps - 1 + drafts, :] = x_ref[r].astype(jnp.float32)
        mixed = bias_ref[...] + weight_ref[0:1, :] * padded[0:drafts, :]
        for k in range(1, taps):
            mixed = mixed + weight_ref[k : k + 1, :] * padded[k : k + drafts, :]
        inputs_ref[r] = (mixed / (1.0 + jnp.exp(-mixed))).astype(jnp.bfloat16)
        for k in range(taps - 1):
            new_pool_ref[slot, k : k + 1, :] = padded[pl.ds(accepted_ref[r] + k, 1), :]
        return 0

    lax.fori_loop(0, count, one, 0)
    pieces, _, depth = proj_ref.shape
    total = None
    for i in range(pieces):
        part = inputs_ref[:, :, i * depth : (i + 1) * depth].reshape(count * drafts, depth)
        term = lax.dot_general(
            proj_ref[i], part, (((1,), (1,)), ((), ())), preferred_element_type=jnp.float32
        )
        total = term if total is None else total + term
    partial_ref[...] = total


def conv_branch(x_part, conv_pool, conv_weight, conv_bias, x_proj, slot, accepted):
    count, drafts, inner = x_part.shape
    return pl.pallas_call(
        conv_kernel,
        out_shape=(
            jax.ShapeDtypeStruct(x_part.shape, jnp.bfloat16),
            jax.ShapeDtypeStruct((x_proj.shape[1], count * drafts), jnp.float32),
            jax.ShapeDtypeStruct(conv_pool.shape, jnp.float32),
        ),
        in_specs=whole(7, smem=2),
        out_specs=tuple(whole(3)),
        scratch_shapes=[pltpu.VMEM((24, inner), jnp.float32)],
        compiler_params=pltpu.CompilerParams(vmem_limit_bytes=VMEM_BYTES),
        cost_estimate=pl.CostEstimate(flops=200_000_000, bytes_accessed=4_000_000, transcendentals=600_000),
    )(slot, accepted, x_part, conv_pool, conv_weight, conv_bias.reshape(1, -1), x_proj)


MESH = pl.DeviceIdType.MESH


def greet(partners):
    barrier = pltpu.get_barrier_semaphore()
    for partner in partners:
        pl.semaphore_signal(barrier, inc=1, device_id=partner, device_id_type=MESH)
    pl.semaphore_wait(barrier, len(partners))


def peers_on(axis, size):
    me = lax.axis_index(axis)
    return [{axis: lax.rem(me + k, size)} for k in range(1, size)]


def gather_kernel(n_mp, n_dp, *refs):
    weights = 4 if n_dp == 8 else 0
    hidden, gain_row = refs[0], refs[1]
    shards = refs[2 : 2 + weights]
    normed = refs[2 + weights]
    wholes = refs[3 + weights : 3 + 2 * weights]
    full, gain, gains, send, recv, local = refs[3 + 2 * weights :]
    m = lax.axis_index("mp")
    width = hidden.shape[1]
    gain[...] = jnp.broadcast_to(gain_row[...].astype(jnp.float32), gain.shape)
    greet(peers_on("mp", n_mp) + (peers_on("dp", n_dp) if weights else []))
    made = []

    def remote(src, dst, target):
        index = len(made)
        copy = pltpu.make_async_remote_copy(
            src_ref=src, dst_ref=dst, send_sem=send.at[index], recv_sem=recv.at[index],
            device_id=target, device_id_type=MESH,
        )
        made.append(copy)
        return copy

    def started(src, dst, target):
        copy = remote(src, dst, target)
        copy.start()
        return copy

    def place(origin):
        start = pl.multiple_of(jnp.clip(origin, 0, n_mp - 1) * width, width)
        return full.at[:, pl.ds(start, width)]

    kept = []

    def keep(src, dst):
        copy = pltpu.make_async_copy(src, dst, local.at[len(kept)])
        copy.start()
        kept.append(copy)

    right, left = jnp.minimum(m + 1, n_mp - 1), jnp.maximum(m - 1, 0)
    steps = n_mp - 1
    relay = []
    for s in range(steps):
        src = hidden if s == 0 else place(m - s)
        ahead = remote(src, place(m - s), {"mp": right})
        src = hidden if s == 0 else place(m + s)
        back = remote(src, place(m + s), {"mp": left})
        relay.append((ahead, back))
    relayed = len(made)

    def sends(s):
        return (m - s >= 0) & (m + 1 < n_mp), (m + s < n_mp) & (m >= 1)

    def gets(s):
        return m - 1 - s >= 0, m + 1 + s < n_mp

    def relay_start(s):
        for copy, go in zip(relay[s], sends(s)):
            pl.when(go)(copy.start)

    def relay_arrive(s):
        for copy, go in zip(relay[s], gets(s)):
            pl.when(go)(copy.wait_recv)

    relay_start(0)
    keep(hidden, place(m))
    keep(gain, gains.at[m])
    if weights:
        d = lax.axis_index("dp")
        other = lambda bit: d + bit - 2 * bit * lax.rem(d // bit, 2)
        core, by_x, by_y = other(1), other(2), other(4)
        diagonal = by_x + 4 - 8 * lax.rem(d // 4, 2)
        own = []
        relayed_weights = (0, 2, 1)
        for w in relayed_weights:
            shard, whole_w = shards[w], wholes[w]
            own.append([started(shard, whole_w.at[d], {"dp": t}) for t in (by_x, by_y, core)])
            keep(shard, whole_w.at[d])
    gain_copies = {
        id(started(gain, gains.at[m], {"mp": lax.rem(m + k, n_mp)})) for k in range(1, n_mp)
    }
    if weights:
        keep(shards[3], wholes[3].at[d])
        for k in range(1, n_dp):
            started(shards[3], wholes[3].at[d], {"dp": lax.rem(d + k, n_dp)})
    relay_arrive(0)
    relay_start(1)
    done = {id(copy) for pair in relay for copy in pair}

    def arrive(copy):
        copy.wait_recv()
        done.add(id(copy))

    if weights:
        halves = []
        for i, w in enumerate(relayed_weights):
            whole_w = wholes[w]
            half = whole_w.shape[1] // 2
            low, high = pl.ds(0, half), pl.ds(half, half)
            arrive(own[i][0])
            first = started(whole_w.at[by_x, low], whole_w.at[by_x, low], {"dp": by_y})
            started(whole_w.at[by_x], whole_w.at[by_x], {"dp": core})
            arrive(own[i][1])
            second = started(whole_w.at[by_y, high], whole_w.at[by_y, high], {"dp": by_x})
            started(whole_w.at[by_y], whole_w.at[by_y], {"dp": core})
            halves.append((first, second))
            if i == 0:
                relay_arrive(1)
                relay_start(2)
        for i, w in enumerate(relayed_weights):
            whole_w = wholes[w]
            half = whole_w.shape[1] // 2
            for copy, part in zip(halves[i], (pl.ds(0, half), pl.ds(half, half))):
                arrive(copy)
                started(whole_w.at[diagonal, part], whole_w.at[diagonal, part], {"dp": core})
    else:
        relay_arrive(1)
        relay_start(2)
    relay_arrive(2)
    kept[0].wait()
    kept[1].wait()
    for copy in made[relayed:]:
        if id(copy) in gain_copies:
            arrive(copy)
    block = 64

    def norm(i, carry):
        rows = pl.ds(pl.multiple_of(i * block, block), block)
        parts = [slice(p * width, (p + 1) * width) for p in range(n_mp)]
        squares = None
        for part in parts:
            values = full[rows, part].astype(jnp.float32)
            term = jnp.sum(values * values, axis=1, keepdims=True)
            squares = term if squares is None else squares + term
        scale = lax.rsqrt(squares / (n_mp * width) + EPS)
        for p, part in enumerate(parts):
            values = full[rows, part].astype(jnp.float32) * scale * gains[p, 0:1, :]
            normed[rows, part] = values.astype(jnp.bfloat16)
        return carry

    lax.fori_loop(0, full.shape[0] // block, norm, 0)
    for copy in made[relayed:]:
        if id(copy) not in done:
            copy.wait_recv()
    for s in range(steps):
        for copy, go in zip(relay[s], sends(s)):
            pl.when(go)(copy.wait_send)
    for copy in made[relayed:]:
        copy.wait_send()
    for copy in kept[2:]:
        copy.wait()


def gather(hidden, gain, weights, n_mp, n_dp):
    tokens, width = hidden.shape
    shapes = [(tokens, n_mp * width)] + [(n_dp,) + w.shape for w in weights]
    anywhere = pl.BlockSpec(memory_space=pl.ANY)
    copies = 2 * (n_mp - 1) + n_mp - 1 + (3 * (3 + 4 + 2) + n_dp - 1 if weights else 0)
    return pl.pallas_call(
        functools.partial(gather_kernel, n_mp, n_dp),
        out_shape=tuple(jax.ShapeDtypeStruct(s, jnp.bfloat16) for s in shapes),
        in_specs=whole(2) + [anywhere] * len(weights),
        out_specs=tuple(whole(1) + [anywhere] * len(weights)),
        scratch_shapes=[
            pltpu.VMEM((tokens, n_mp * width), jnp.bfloat16),
            pltpu.VMEM((8, width), jnp.float32),
            pltpu.VMEM((n_mp, 8, width), jnp.float32),
            pltpu.SemaphoreType.DMA((copies,)),
            pltpu.SemaphoreType.DMA((copies,)),
            pltpu.SemaphoreType.DMA((2 + len(weights),)),
        ],
        compiler_params=pltpu.CompilerParams(
            collective_id=0, has_side_effects=True, vmem_limit_bytes=16 * 1024 * 1024
        ),
        cost_estimate=pl.CostEstimate(flops=0, bytes_accessed=100_000_000, transcendentals=0),
    )(hidden, gain.reshape(1, -1), *weights)


def sum_kernel(
    n_mp, partial_ref, normed_ref, weight_ref, packed_ref, z_ref, sent, landed, total_ref, send, recv
):
    m = lax.axis_index("mp")
    columns_all, tokens = partial_ref.shape
    rows = tokens // n_mp
    blocks = 4
    width = weight_ref.shape[1] // blocks

    def gate(block):
        columns = slice(block * width, (block + 1) * width)
        product = jnp.dot(normed_ref[...], weight_ref[:, columns], preferred_element_type=jnp.float32)
        z_ref[:, columns] = product.astype(jnp.bfloat16)

    greet(peers_on("mp", n_mp))
    copies = []
    for k in range(1, n_mp):
        target = lax.rem(m + k, n_mp)
        piece = partial_ref[:, pl.ds(pl.multiple_of(target * rows, rows), rows)]
        sent[k - 1] = piece.astype(jnp.bfloat16)
        copy = pltpu.make_async_remote_copy(
            src_ref=sent.at[k - 1], dst_ref=landed.at[k - 1], send_sem=send.at[k - 1],
            recv_sem=recv.at[k - 1], device_id={"mp": target}, device_id_type=MESH,
        )
        copy.start()
        copies.append(copy)
    for block in range(blocks // 2):
        gate(block)
    mine = pl.ds(pl.multiple_of(m * rows, rows), rows)
    total = partial_ref[:, mine]
    for k in range(1, n_mp):
        copies[k - 1].wait_recv()
        total = total + landed[k - 1].astype(jnp.float32)
    total_ref[:, mine] = total.astype(jnp.bfloat16)
    spread = []
    for k in range(1, n_mp):
        copy = pltpu.make_async_remote_copy(
            src_ref=total_ref.at[:, mine], dst_ref=total_ref.at[:, mine],
            send_sem=send.at[n_mp - 2 + k], recv_sem=recv.at[n_mp - 2 + k],
            device_id={"mp": lax.rem(m + k, n_mp)}, device_id_type=MESH,
        )
        copy.start()
        spread.append(copy)
    for block in range(blocks // 2, blocks):
        gate(block)
    for copy in spread:
        copy.wait_recv()
    packed_ref[:, :columns_all] = total_ref[...].astype(jnp.float32).T.astype(jnp.bfloat16)
    for copy in copies + spread:
        copy.wait_send()


def sum_and_gate(partial, normed, z_weight, n_mp):
    columns, rows = partial.shape
    return pl.pallas_call(
        functools.partial(sum_kernel, n_mp),
        out_shape=(
            jax.ShapeDtypeStruct((rows, columns), jnp.bfloat16),
            jax.ShapeDtypeStruct((rows, z_weight.shape[1]), jnp.bfloat16),
        ),
        in_specs=whole(3),
        out_specs=tuple(whole(2)),
        scratch_shapes=[
            pltpu.VMEM((n_mp - 1, columns, rows // n_mp), jnp.bfloat16),
            pltpu.VMEM((n_mp - 1, columns, rows // n_mp), jnp.bfloat16),
            pltpu.VMEM((columns, rows), jnp.bfloat16),
            pltpu.SemaphoreType.DMA((2 * (n_mp - 1),)),
            pltpu.SemaphoreType.DMA((2 * (n_mp - 1),)),
        ],
        compiler_params=pltpu.CompilerParams(
            collective_id=1, has_side_effects=True, vmem_limit_bytes=VMEM_BYTES
        ),
        cost_estimate=pl.CostEstimate(flops=2_000_000_000, bytes_accessed=30_000_000, transcendentals=0),
    )(partial, normed, z_weight)


def scan_kernel(
    n_mp, n_dp, shift_ref, class_ref, slot_ref, accepted_ref, holder_ref,
    low_ref, dt_proj_ref, dt_bias_ref, a_log_ref, skip_ref, inputs_ref, z_ref, pool_ref,
    proj_ref, hidden_ref,
    out_ref, new_pool_ref,
    decay, delta, drive, scanned, kept_ref, gated,
    sent, landed, relay_out, relay_in, far_own, far_sent, far_landed, total, rows, outgoing, incoming,
    send, recv, relay_send, relay_recv, far_send, far_recv, route_send, route_recv,
):
    m, d = lax.axis_index("mp"), lax.axis_index("dp")
    width = hidden_ref.shape[1]
    capacity, period, drafts, _ = rows.shape
    states, inner = a_log_ref.shape
    rank = dt_proj_ref.shape[0]
    part = 512
    chunk = period * drafts
    greet(peers_on("mp", n_mp) + peers_on("dp", n_dp))
    decay[...] = -jnp.exp(a_log_ref[...])

    def scan_one(r, where):
        slot = slot_ref[r]
        last = accepted_ref[r] - 1
        packed = low_ref[r]
        raw = jnp.dot(packed[:, :rank], dt_proj_ref[...], preferred_element_type=jnp.float32)
        raw = raw + dt_bias_ref[...]
        step = jnp.maximum(raw, 0.0) + jnp.log1p(jnp.exp(-jnp.abs(raw)))
        delta[...] = step
        drive[...] = step * inputs_ref[r].astype(jnp.float32)
        both = packed[:, rank : rank + 2 * states].astype(jnp.float32).T
        pieces = [slice(i, i + part) for i in range(0, inner, part)]
        state = [pool_ref[slot, :, lanes] for lanes in pieces]
        kept = list(state)
        for t in range(drafts):
            column = jnp.broadcast_to(both[:, t : t + 1], (2 * states, part))
            b_wide, c_wide = column[:states], column[states:]
            chosen = last == t
            for i, lanes in enumerate(pieces):
                grown = jnp.exp(delta[t : t + 1, lanes] * decay[:, lanes]) * state[i]
                state[i] = grown + drive[t : t + 1, lanes] * b_wide
                scanned[t : t + 1, lanes] = jnp.sum(state[i] * c_wide, axis=0, keepdims=True)
                kept[i] = jnp.where(chosen, state[i], kept[i])
        for i, lanes in enumerate(pieces):
            kept_ref[r, :, lanes] = kept[i]
        z = z_ref[r].astype(jnp.float32)
        mixed = scanned[...] + skip_ref[...] * inputs_ref[r].astype(jnp.float32)
        gated[where] = (mixed * (z / (1.0 + jnp.exp(-z)))).astype(jnp.bfloat16)

    def share(target):
        columns = pl.ds(pl.multiple_of(target * width, width), width)
        flat = gated[...].reshape(chunk, inner)
        return jnp.dot(flat, proj_ref[:, columns], preferred_element_type=jnp.float32)

    partner = m + 1 - 2 * lax.rem(m, 2)
    far = 2 - 2 * (m // 2)
    is_end = (m == 0) | (m == n_mp - 1)
    is_inner = (m > 0) & (m < n_mp - 1)
    copies, relays, fars = [], [], []

    def remote(src, dst, send_sem, recv_sem, target):
        return pltpu.make_async_remote_copy(
            src_ref=src, dst_ref=dst, send_sem=send_sem, recv_sem=recv_sem,
            device_id={"mp": target}, device_id_type=MESH,
        )

    def pass_on(c):
        @pl.when(is_inner)
        def _():
            for j in range(2):
                relays[c][j].wait_recv()
                mixed = far_own[c % 2, j] + relay_in[c, j].astype(jnp.float32)
                far_sent[c, j] = mixed.astype(jnp.bfloat16)
                fars[c][j].start()

    for c in range(capacity):

        def one(k, carry, c=c):
            scan_one(c * period + k, k)
            return carry

        lax.fori_loop(0, period, one, 0)
        relays.append([
            remote(relay_out.at[c, j], relay_in.at[c, j], relay_send.at[c, j], relay_recv.at[c, j], partner)
            for j in range(2)
        ])
        fars.append([
            remote(far_sent.at[c, j], far_landed.at[c], far_send.at[c, j], far_recv.at[c], far + j)
            for j in range(2)
        ])
        for j in range(2):
            far_own[c % 2, j] = share(far + j)

            @pl.when(is_end)
            def _():
                relay_out[c, j] = far_own[c % 2, j].astype(jnp.bfloat16)
                relays[c][j].start()

        sent[c] = share(partner).astype(jnp.bfloat16)
        copies.append(remote(sent.at[c], landed.at[c], send.at[c], recv.at[c], partner))
        copies[c].start()
        own = hidden_ref[c * chunk : (c + 1) * chunk, :].astype(jnp.float32)
        total[c] = share(m) + own
        if c > 0:
            pass_on(c - 1)
    pass_on(capacity - 1)

    def settle(s, carry):
        holder = holder_ref[s]
        kept = kept_ref[jnp.maximum(holder, 0)]
        new_pool_ref[s] = jnp.where(holder >= 0, kept, pool_ref[s])
        return carry

    lax.fori_loop(0, new_pool_ref.shape[0], settle, 0)
    routed = []
    for c in range(capacity):
        copies[c].wait_recv()
        fars[c][0].wait_recv()
        layer = total[c] + landed[c].astype(jnp.float32) + far_landed[c].astype(jnp.float32)
        rows[c] = layer.astype(jnp.bfloat16).reshape(period, drafts, width)
        for o in range(n_dp):
            if o == 0:
                incoming[c, 0] = rows[c, class_ref[0]]
                continue
            outgoing[c, o] = rows[c, class_ref[o]]
            index = c * (n_dp - 1) + o - 1
            copy = pltpu.make_async_remote_copy(
                src_ref=outgoing.at[c, o], dst_ref=incoming.at[c, o], send_sem=route_send.at[index],
                recv_sem=route_recv.at[index], device_id={"dp": lax.rem(d + o, n_dp)},
                device_id_type=MESH,
            )
            copy.start()
            routed.append(copy)
    for copy in routed:
        copy.wait_recv()
    for c in range(capacity):
        for k in range(period):
            out_ref[c * period + k] = incoming[c, shift_ref[k]]
    for copy in copies + routed:
        copy.wait_send()
    for c in range(capacity):
        for j in range(2):
            pl.when(is_end)(relays[c][j].wait_send)
            pl.when(is_inner)(fars[c][j].wait_send)


def scan_and_output(
    low, dt_proj, dt_bias, a_log, skip, inputs, z_part, state_pool, out_proj, hidden,
    permutation, slot, accepted, n_mp, n_dp,
):
    tokens, width = hidden.shape
    count, drafts, inner = inputs.shape
    states, slots = a_log.shape[0], state_pool.shape[0]
    period = min(count, n_dp)
    capacity = count // period
    shift = (permutation[:period] // count - lax.axis_index("dp") + n_dp) % n_dp
    klass = jnp.argmax(jnp.arange(n_dp)[:, None] == shift[None, :], axis=1).astype(jnp.int32)
    held = slot[None, :] == jnp.arange(slots)[:, None]
    holder = jnp.max(jnp.where(held, jnp.arange(count)[None, :], -1), axis=1).astype(jnp.int32)
    box = (capacity, n_dp, drafts, width)
    piece = (period * drafts, width)
    routes = capacity * (n_dp - 1)
    return pl.pallas_call(
        functools.partial(scan_kernel, n_mp, n_dp),
        out_shape=(
            jax.ShapeDtypeStruct((count, drafts, width), jnp.bfloat16),
            jax.ShapeDtypeStruct(state_pool.shape, jnp.float32),
        ),
        in_specs=whole(15, smem=5),
        out_specs=tuple(whole(2)),
        scratch_shapes=[
            pltpu.VMEM((states, inner), jnp.float32),
            pltpu.VMEM((drafts, inner), jnp.float32),
            pltpu.VMEM((drafts, inner), jnp.float32),
            pltpu.VMEM((drafts, inner), jnp.float32),
            pltpu.VMEM((count, states, inner), jnp.float32),
            pltpu.VMEM((period, drafts, inner), jnp.bfloat16),
            pltpu.VMEM((capacity,) + piece, jnp.bfloat16),
            pltpu.VMEM((capacity,) + piece, jnp.bfloat16),
            pltpu.VMEM((capacity, 2) + piece, jnp.bfloat16),
            pltpu.VMEM((capacity, 2) + piece, jnp.bfloat16),
            pltpu.VMEM((2, 2) + piece, jnp.float32),
            pltpu.VMEM((capacity, 2) + piece, jnp.bfloat16),
            pltpu.VMEM((capacity,) + piece, jnp.bfloat16),
            pltpu.VMEM((capacity, period * drafts, width), jnp.float32),
            pltpu.VMEM((capacity, period, drafts, width), jnp.bfloat16),
            pltpu.VMEM(box, jnp.bfloat16),
            pltpu.VMEM(box, jnp.bfloat16),
            pltpu.SemaphoreType.DMA((capacity,)),
            pltpu.SemaphoreType.DMA((capacity,)),
            pltpu.SemaphoreType.DMA((capacity, 2)),
            pltpu.SemaphoreType.DMA((capacity, 2)),
            pltpu.SemaphoreType.DMA((capacity, 2)),
            pltpu.SemaphoreType.DMA((capacity,)),
            pltpu.SemaphoreType.DMA((routes,)),
            pltpu.SemaphoreType.DMA((routes,)),
        ],
        compiler_params=pltpu.CompilerParams(
            collective_id=2, has_side_effects=True, vmem_limit_bytes=VMEM_BYTES
        ),
        cost_estimate=pl.CostEstimate(
            flops=3_000_000_000, bytes_accessed=150_000_000, transcendentals=9_000_000
        ),
    )(
        shift.astype(jnp.int32), klass, slot, accepted, holder,
        low, dt_proj, dt_bias.reshape(1, -1), a_log, skip.reshape(1, -1),
        inputs, z_part, state_pool, out_proj, hidden,
    )


def on_device(
    hidden, norm_gain, in_x, in_z, conv_weight, conv_bias, x_proj, dt_proj, dt_bias,
    a_log, skip, out_proj, state_pool, conv_pool, permutation, page_table, accepted,
):
    count, drafts, width_local = hidden.shape
    tokens = count * drafts
    inner_local = in_x.shape[1]
    slot = page_table % state_pool.shape[0]
    n_dp, n_mp = lax.axis_size("dp"), lax.axis_size("mp")
    flat_hidden = hidden.reshape(tokens, width_local)

    if n_dp == 8:
        weights = (in_x, in_z, x_proj.T, dt_proj)
        normed, *weights = gather(flat_hidden, norm_gain, weights, n_mp, n_dp)
        x_weight, z_weight, _, dt_proj = [w.reshape(-1, w.shape[2]) for w in weights]
        x_proj = weights[2]
    else:
        normed, = gather(flat_hidden, norm_gain, (), n_mp, n_dp)
        x_weight, z_weight, x_proj, dt_proj = [
            lax.all_gather(w, "dp", axis=0, tiled=True) for w in (in_x, in_z, x_proj, dt_proj)
        ]
        x_proj = x_proj.T[None]
    out_proj, normed = lax.optimization_barrier((out_proj, normed))
    out_proj = lax.all_gather(out_proj, "dp", axis=1, tiled=True)

    x_part = jnp.dot(normed, x_weight, preferred_element_type=jnp.float32).astype(jnp.bfloat16)
    x_part = x_part.reshape(count, drafts, inner_local)

    inputs, partial, new_conv_pool = conv_branch(
        x_part, conv_pool, conv_weight, conv_bias, x_proj, slot, accepted
    )
    summed, z_part = sum_and_gate(partial, normed, z_weight, n_mp)
    verified, new_state_pool = scan_and_output(
        summed.reshape(count, drafts, -1), dt_proj, dt_bias, a_log, skip, inputs,
        z_part.reshape(count, drafts, inner_local), state_pool, out_proj, flat_hidden,
        permutation, slot, accepted, n_mp, n_dp,
    )
    return (verified, new_state_pool, new_conv_pool)


def solution(mesh):
    return jax.shard_map(
        on_device,
        mesh=mesh,
        in_specs=(
            P("dp", None, "mp"),
            P("mp"),
            P("dp", "mp"),
            P("dp", "mp"),
            P(None, "mp"),
            P("mp"),
            P(("mp", "dp"), None),
            P("dp", "mp"),
            P("mp"),
            P(None, "mp"),
            P("mp"),
            P("mp", "dp"),
            P("dp", None, "mp"),
            P("dp", None, "mp"),
            P("dp"),
            P("dp"),
            P("dp"),
        ),
        out_specs=(P("dp", None, "mp"), P("dp", None, "mp"), P("dp", None, "mp")),
        check_vma=False,
    )
```
